32 devices in a mesh: gx: 8 (over z, core), gy: 4 (over y, x).
Axes of the slice: x: 2, y: 2, z: 4, core: 2. Of those that a mesh axis runs over, the one named last changes fastest.
Arguments:
- pdf_old: float32 [4096, 19, 256], P(('gx', 'gy')), may hold values from -3 to 3
- tile_target: int32 [4096], P(('gx', 'gy')), may hold values from 0 to 4095, as said below
- porosity: float32 [128, 64, 128], P(('gx', 'gy')), may hold values from 0 to 0.6
- relaxation: float32 [128, 64, 128], P(('gx', 'gy')), may hold values from 0.6 to 1.8
- solid_mask: int32 [128, 64, 128], P('gx', 'gy'), may hold values 0 or 1
- force: float32 [3], replicated, may hold values from -0.1 to 0.1
Outputs:
- deviation_out: float32 [19, 128, 64, 128], P(None, 'gx', 'gy')
The draws below stay inside these ranges and needn't reach their ends.
Inputs may be any that keep to these rules, and one draw needn't show every extreme that they name: tile_target holds every tile index once. The tiles of one device go to at most 8 of their number to any one device (device = tile index // 128), and in every draw some device sends exactly 8 tiles to some device.
All inputs are finite; a program needn't handle non-finite values. No bound on the sum of `solid_mask` on one device may be relied on, other than what follows from the above.
Results may differ from the reference program's by a relative error of at most 0.00023.
Values sent between devices are 32-bit elements; how exact they have to be, the bound alone decides.
A program may use at most 64 MiB of HBM per device.

```python
import jax
import jax.numpy as jnp
import numpy as np
from jax import lax

CX = 16
CY = 16
NZ = 128
TY = 2
STEPS = 2
NX = 128
NY = 64
TILES_DEV = 128
TILES = 4096
TILE_CELLS = 256
N_GX = 8
N_GY = 4


def draw_tile_target(key, part):
    dev_count = TILES // TILES_DEV
    capacity = 2 * TILES_DEV // dev_count
    half_cap = capacity // 2
    key_list = jax.random.split(key, 5)
    spread = jax.random.randint(key_list[0], (dev_count // 2,), 0, half_cap + 1).at[0].set(half_cap)
    multiple = jnp.stack([half_cap + spread, half_cap - spread], axis=1).reshape(dev_count)
    offsets = jnp.repeat(jnp.arange(dev_count), multiple, total_repeat_length=TILES_DEV)
    perm_first = jax.random.permutation(key_list[1], dev_count)
    perm_second = jax.random.permutation(key_list[2], dev_count)
    owner_dev = perm_second[(perm_first[:, None] + offsets[None, :]) % dev_count]
    orders = jax.vmap(lambda subkey: jax.random.permutation(subkey, TILES_DEV))(jax.random.split(key_list[3], dev_count))
    slot_ids = orders[owner_dev, jnp.arange(TILES_DEV)[None, :]]
    targets = owner_dev * TILES_DEV + slot_ids
    shuffle = jax.vmap(lambda subkey: jax.random.permutation(subkey, TILES_DEV))(jax.random.split(key_list[4], dev_count))
    targets = jnp.take_along_axis(targets, shuffle, axis=1)
    return targets.reshape(TILES).astype(jnp.int32)


def touch_ends(result, key, smallest, high):
    spot = [jax.random.randint(jax.random.fold_in(key, axis), (), 0, length) for axis, length in enumerate(result.shape)]
    widest = result.shape.index(max(result.shape))
    next_to = spot[:widest] + [(spot[widest] + 1) % result.shape[widest]] + spot[widest + 1:]
    return result.at[tuple(spot)].set(smallest).at[tuple(next_to)].set(high)


def shard_levels(rng, dims, shards, low, top_value):
    factor_of = 1.0
    for position, parts in shards:
        steps = jax.random.uniform(jax.random.fold_in(jax.random.fold_in(rng, 6), position), (parts,), jnp.float32, low / len(shards), top_value / len(shards))
        factor_of = factor_of * jnp.repeat(jnp.exp(steps), dims[position] // parts).reshape((-1,) + (1,) * (len(dims) - 1 - position))
    return factor_of


def centred(key, extent, scale, reach, cuts=(), dtype=jnp.bfloat16):
    entries = scale * jax.random.normal(key, extent, jnp.float32)
    if cuts:
        entries = entries * shard_levels(key, extent, cuts, -0.22, 0.18)
    return jnp.clip(entries, -reach, reach).astype(dtype)


def setup_inputs(seed: int = 0) -> dict:
    splits = jax.random.split(jax.random.key(seed), 7)
    pdf_old = centred(splits[0], (TILES, 19, TILE_CELLS), 0.5, 3.0, ((0, 32),), jnp.float32)
    tile_target = draw_tile_target(jax.random.fold_in(splits[6], 71), 0)
    porosity = jnp.clip(0.6 * jax.random.uniform(splits[2], (NX, NY, NZ), jnp.float32) ** shard_levels(splits[2], (NX, NY, NZ), ((0, 32),), -0.2, 0.2), 0.0, 0.6)
    relaxation = jnp.clip(0.6 + 1.1999999 * jax.random.uniform(splits[3], (NX, NY, NZ), jnp.float32) ** shard_levels(splits[3], (NX, NY, NZ), ((0, 32),), -0.2, 0.2), 0.6, 1.8)
    solid_mask = touch_ends((jax.random.randint(splits[4], (NX, NY, NZ), 0, 10) < 3).astype(jnp.int32), jax.random.fold_in(splits[4], 1), 0, 1)
    force = jnp.clip(jax.random.uniform(splits[5], (3,), jnp.float32, -0.1, 0.1), -0.1, 0.1)
    return dict(pdf_old=pdf_old, tile_target=tile_target, porosity=porosity, relaxation=relaxation, solid_mask=solid_mask, force=force)


VELOCITY = ((0, 0, 0), (1, 0, 0), (-1, 0, 0), (0, 1, 0), (0, -1, 0), (0, 0, 1), (0, 0, -1),
            (1, 1, 0), (-1, -1, 0), (1, -1, 0), (-1, 1, 0), (1, 0, 1), (-1, 0, -1),
            (1, 0, -1), (-1, 0, 1), (0, 1, 1), (0, -1, -1), (0, 1, -1), (0, -1, 1))
OPPOSITE = [0, 2, 1, 4, 3, 6, 5, 8, 7, 10, 9, 12, 11, 14, 13, 16, 15, 18, 17]
WEIGHT_LIST = [1.0 / 3.0] + [1.0 / 18.0] * 6 + [1.0 / 36.0] * 12
MAGIC = 0.1875


def lattice_weights(ndim):
    return jnp.array(WEIGHT_LIST, jnp.float32).reshape((19,) + (1,) * (ndim - 1))


def component(dist, axis_pos):
    plus_set = np.array([index for index in range(19) if VELOCITY[index][axis_pos] == 1])
    minus_set = np.array([index for index in range(19) if VELOCITY[index][axis_pos] == -1])
    return jnp.sum(dist[plus_set], axis=0) - jnp.sum(dist[minus_set], axis=0)


def collide(dist, porosity, omega_plus, solid_mask, force):
    weights = lattice_weights(dist.ndim)
    density = jnp.sum(dist, axis=0)
    flow = [component(dist, axis_pos) + 0.5 * force[axis_pos] for axis_pos in range(3)]
    speed_sq = flow[0] * flow[0] + flow[1] * flow[1] + flow[2] * flow[2]
    along = jnp.stack([VELOCITY[index][0] * flow[0] + VELOCITY[index][1] * flow[1] + VELOCITY[index][2] * flow[2] for index in range(19)])
    push = jnp.stack([VELOCITY[index][0] * force[0] + VELOCITY[index][1] * force[1] + VELOCITY[index][2] * force[2] for index in range(19)])
    push = push.reshape((19,) + (1,) * (dist.ndim - 1))
    reversed_dist = dist[np.array(OPPOSITE)]
    even_part = 0.5 * (dist + reversed_dist)
    odd_part = 0.5 * (dist - reversed_dist)
    eq_even = weights * (density + 4.5 * along * along - 1.5 * speed_sq)
    eq_odd = 3.0 * weights * along
    omega_minus = 1.0 / (MAGIC / (1.0 / omega_plus - 0.5) + 0.5)
    relaxed = dist - omega_plus * (even_part - eq_even) - omega_minus * (odd_part - eq_odd) + 3.0 * weights * push
    solid = porosity + solid_mask.astype(jnp.float32) * (1.0 - porosity)
    return (1.0 - solid) * relaxed + solid * reversed_dist


def reference(pdf_old, tile_target, porosity, relaxation, solid_mask, force):
    placed = jnp.zeros_like(pdf_old).at[tile_target].set(pdf_old)
    deviation = placed.reshape(N_GX, N_GY, CX, CY // TY, 19, TY, NZ).transpose(4, 0, 2, 1, 3, 5, 6).reshape(19, NX, NY, NZ)
    weights = lattice_weights(4)
    dist = weights * (1.0 + deviation)
    for step_index in range(STEPS):
        def plane_collide(items):
            return collide(items[0], items[1], items[2], items[3], force)

        post = lax.map(plane_collide, (jnp.moveaxis(dist, 1, 0), porosity, relaxation, solid_mask))
        post = jnp.moveaxis(post, 0, 1)
        dist = jnp.stack([jnp.roll(post[index], VELOCITY[index], axis=(0, 1, 2)) for index in range(19)])
    return dist / weights - 1.0
```

```python
import functools

import jax
import jax.numpy as jnp
from jax import lax
from jax.experimental import pallas as pl
from jax.experimental.pallas import tpu as pltpu
from jax.sharding import PartitionSpec as P

STEPS = 2
VELOCITY = (
    (0, 0, 0),
    (1, 0, 0),
    (-1, 0, 0),
    (0, 1, 0),
    (0, -1, 0),
    (0, 0, 1),
    (0, 0, -1),
    (1, 1, 0),
    (-1, -1, 0),
    (1, -1, 0),
    (-1, 1, 0),
    (1, 0, 1),
    (-1, 0, -1),
    (1, 0, -1),
    (-1, 0, 1),
    (0, 1, 1),
    (0, -1, -1),
    (0, 1, -1),
    (0, -1, 1),
)
MAGIC = 0.1875
MESH = pl.DeviceIdType.MESH
LANES = 128
PAD = 8
MIB = 1 << 20


def moving(axis, sign):
    return [q for q in range(19) if VELOCITY[q][axis] == sign]


CORNERS = [(q, VELOCITY[q][0], VELOCITY[q][1]) for q in range(19) if VELOCITY[q][0] * VELOCITY[q][1] != 0]


def collide(dev, porosity, omega, mask, force):
    solid = porosity + mask.astype(jnp.float32) * (1.0 - porosity)
    fluid = 1.0 - solid
    omega_minus = (2.0 - omega) / (1.0 + (2.0 * MAGIC - 0.5) * omega)
    sums = {q: dev[q] + dev[q + 1] for q in range(1, 19, 2)}
    gaps = {q: dev[q] - dev[q + 1] for q in range(1, 19, 2)}
    axis_sum = sums[1] + sums[3] + sums[5]
    diagonal_sum = (sums[7] + sums[9]) + (sums[11] + sums[13]) + (sums[15] + sums[17])
    density = dev[0] * (1.0 / 3.0) + axis_sum * (1.0 / 18.0) + diagonal_sum * (1.0 / 36.0)
    flow = []
    for axis in range(3):
        straight = gaps[1 + 2 * axis]
        slanted = None
        for q in range(7, 19, 2):
            if VELOCITY[q][axis]:
                term = gaps[q] if VELOCITY[q][axis] > 0 else -gaps[q]
                slanted = term if slanted is None else slanted + term
        flow.append(straight * (1.0 / 18.0) + slanted * (1.0 / 36.0) + 0.5 * force[axis])
    base = density - 1.5 * (flow[0] * flow[0] + flow[1] * flow[1] + flow[2] * flow[2])
    pull = fluid * omega
    keep = 0.5 * (1.0 - pull)
    turn = 0.5 * (fluid * (1.0 - omega_minus) - solid)
    push = [3.0 * fluid * (omega_minus * flow[axis] + force[axis]) for axis in range(3)]

    def along(vector, velocity):
        total = None
        for axis in range(3):
            if velocity[axis]:
                term = vector[axis] if velocity[axis] > 0 else -vector[axis]
                total = term if total is None else total + term
        return total

    post = [None] * 19
    post[0] = dev[0] + pull * (base - dev[0])
    for q in range(1, 19, 2):
        speed = along(flow, VELOCITY[q])
        even = keep * sums[q] + pull * (base + 4.5 * (speed * speed))
        odd = turn * gaps[q] + along(push, VELOCITY[q])
        post[q] = even + odd
        post[q + 1] = even - odd
    return post


def pack_kernel(held, capacity, parts, target, pdf, packed, labels, count, halves, sems):
    depth = parts * capacity
    copies = [
        pltpu.make_async_copy(
            pdf.at[:, :, pl.ds(r * LANES, LANES)], halves.at[r], sems.at[r]
        )
        for r in range(parts)
    ]
    for copy in copies:
        copy.start()
    owners = packed.shape[0]
    labels[...] = jnp.full(labels.shape, -1, jnp.int32)

    def clear(d, carry):
        count[d] = 0
        return carry

    lax.fori_loop(0, owners, clear, 0)
    for copy in copies:
        copy.wait()
    flat = [halves.at[r].reshape(19 * held, LANES) for r in range(parts)]

    def place(k, carry):
        goal = target[k]
        owner = lax.div(goal, held)
        rank = count[owner]
        count[owner] = rank + 1
        labels[owner, pl.ds(rank, 1), :] = jnp.full((1, LANES), goal - owner * held, jnp.int32)
        for r in range(parts):
            packed[owner, pl.ds(rank * parts + r, 19, stride=depth), :] = flat[r][
                pl.ds(k, 19, stride=held), :
            ]
        return carry

    lax.fori_loop(0, held, place, 0)


def pack(target, pdf, owners, capacity, parts):
    held = pdf.shape[1]
    return pl.pallas_call(
        functools.partial(pack_kernel, held, capacity, parts),
        out_shape=(
            jax.ShapeDtypeStruct((owners, 19 * capacity * parts, LANES), jnp.float32),
            jax.ShapeDtypeStruct((owners, capacity, LANES), jnp.int32),
        ),
        in_specs=[pl.BlockSpec(memory_space=pltpu.SMEM), pl.BlockSpec(memory_space=pl.ANY)],
        out_specs=[pl.BlockSpec(memory_space=pltpu.VMEM)] * 2,
        scratch_shapes=[
            pltpu.SMEM((owners,), jnp.int32),
            pltpu.VMEM((parts, 19, held, LANES), jnp.float32),
            pltpu.SemaphoreType.DMA((parts,)),
        ],
        compiler_params=pltpu.CompilerParams(vmem_limit_bytes=32 * MIB),
        name="pack_tiles",
    )(target, pdf)


def exchange_kernel(nx, ny, packed, labels, poro, relax, arrived, places, poro_block, relax_block,
                    tile_send, tile_recv, label_send, label_recv, cell_send, cell_recv, own):
    n = nx * ny
    a, b = lax.axis_index("gx"), lax.axis_index("gy")
    me = a * ny + b
    slab = poro.shape[0]
    width = poro.shape[1] // ny
    barrier = pltpu.get_barrier_semaphore()

    def greet(o, carry):
        t = lax.rem(me + o, n)
        pl.semaphore_signal(barrier, inc=1, device_id=(t // ny, lax.rem(t, ny)), device_id_type=MESH)
        return carry

    lax.fori_loop(1, n, greet, 0)
    pl.semaphore_wait(barrier, n - 1)

    def tile_copies(o, source, target):
        device = (target // ny, lax.rem(target, ny))
        return (
            pltpu.make_async_remote_copy(
                src_ref=labels.at[target], dst_ref=places.at[source],
                send_sem=label_send.at[o], recv_sem=label_recv.at[o],
                device_id=device, device_id_type=MESH,
            ),
            pltpu.make_async_remote_copy(
                src_ref=packed.at[target], dst_ref=arrived.at[source],
                send_sem=tile_send.at[o], recv_sem=tile_recv.at[o],
                device_id=device, device_id_type=MESH,
            ),
        )

    def cell_copies(o, source, target):
        return [
            pltpu.make_async_remote_copy(
                src_ref=whole.at[:, pl.ds(target * width, width), :],
                dst_ref=block.at[pl.ds(source * slab, slab)],
                send_sem=cell_send.at[2 * o + i], recv_sem=cell_recv.at[2 * o + i],
                device_id=(a, target), device_id_type=MESH,
            )
            for i, (whole, block) in enumerate(((poro, poro_block), (relax, relax_block)))
        ]

    def send_tiles(o, carry):
        for copy in tile_copies(o, me, lax.rem(me + o, n)):
            copy.start()
        return carry

    lax.fori_loop(1, n, send_tiles, 0)
    for o in range(1, ny):
        for copy in cell_copies(o, b, lax.rem(b + o, ny)):
            copy.start()
    mine = [
        pltpu.make_async_copy(labels.at[me], places.at[me], own.at[0]),
        pltpu.make_async_copy(packed.at[me], arrived.at[me], own.at[1]),
        pltpu.make_async_copy(
            poro.at[:, pl.ds(b * width, width), :], poro_block.at[pl.ds(b * slab, slab)], own.at[2]
        ),
        pltpu.make_async_copy(
            relax.at[:, pl.ds(b * width, width), :], relax_block.at[pl.ds(b * slab, slab)], own.at[3]
        ),
    ]
    for copy in mine:
        copy.start()
    for copy in mine:
        copy.wait()
    for o in range(1, ny):
        for copy in cell_copies(o, lax.rem(b + ny - o, ny), lax.rem(b + o, ny)):
            copy.wait_send()
            copy.wait_recv()

    def take_tiles(o, carry):
        for copy in tile_copies(o, lax.rem(me + n - o, n), lax.rem(me + o, n)):
            copy.wait_send()
            copy.wait_recv()
        return carry

    lax.fori_loop(1, n, take_tiles, 0)


def exchange(packed, labels, poro, relax, nx, ny, block):
    n = nx * ny
    return pl.pallas_call(
        functools.partial(exchange_kernel, nx, ny),
        out_shape=(
            jax.ShapeDtypeStruct(packed.shape, jnp.float32),
            jax.ShapeDtypeStruct(labels.shape, jnp.int32),
            jax.ShapeDtypeStruct(block, jnp.float32),
            jax.ShapeDtypeStruct(block, jnp.float32),
        ),
        in_specs=[pl.BlockSpec(memory_space=pl.ANY)] * 4,
        out_specs=[pl.BlockSpec(memory_space=pl.ANY)] * 4,
        scratch_shapes=[pltpu.SemaphoreType.DMA((n,))] * 4
        + [pltpu.SemaphoreType.DMA((2 * ny,))] * 2
        + [pltpu.SemaphoreType.DMA((4,))],
        compiler_params=pltpu.CompilerParams(collective_id=0, has_side_effects=True),
        name="exchange_tiles",
    )(packed, labels, poro, relax)


def first_kernel(capacity, parts, source, row, force, arrived, poro, relax, mask, post, plane):
    bx, by = poro.shape[:2]
    depth = capacity * parts
    strips = by // parts
    forces = [force[axis] for axis in range(3)]

    def step(x, carry):
        for j in range(strips):
            s = x * strips + j
            for r in range(parts):
                plane[pl.ds(j * parts + r, 19, stride=by), :] = arrived[
                    source[s], pl.ds(row[s] + r, 19, stride=depth), :
                ]
        for h in range(0, by, 8):
            dev = [plane[q * by + h : q * by + h + 8, :] for q in range(19)]
            done = collide(dev, poro[x, h : h + 8], relax[x, h : h + 8], mask[x, h : h + 8], forces)
            for q in range(19):
                post[q, x, h : h + 8, :] = done[q]
        return carry

    lax.fori_loop(0, bx, step, 0)


def first_collision(source, row, force, arrived, poro, relax, mask, capacity, parts):
    bx, by, nz = poro.shape
    return pl.pallas_call(
        functools.partial(first_kernel, capacity, parts),
        out_shape=jax.ShapeDtypeStruct((19, bx, by, nz), jnp.float32),
        in_specs=[pl.BlockSpec(memory_space=pltpu.SMEM)] * 3
        + [pl.BlockSpec(memory_space=pltpu.VMEM)] * 4,
        out_specs=pl.BlockSpec(memory_space=pltpu.VMEM),
        scratch_shapes=[pltpu.VMEM((19 * by, LANES), jnp.float32)],
        compiler_params=pltpu.CompilerParams(vmem_limit_bytes=32 * MIB),
        name="place_and_collide",
    )(source, row, force, arrived, poro, relax, mask)


def steps_kernel(nx, ny, force, post, poro, relax, mask, out, first, second,
                 x_send, y_send, c_send, x_recv, y_recv, c_recv, send, recv, own):
    bx, by = poro.shape[:2]
    a, b = lax.axis_index("gx"), lax.axis_index("gy")
    ring_x = {1: lax.rem(a + 1, nx), -1: lax.rem(a + nx - 1, nx), 0: a}
    ring_y = {1: lax.rem(b + 1, ny), -1: lax.rem(b + ny - 1, ny), 0: b}
    inner = post.at[...]
    load = pltpu.make_async_copy(inner, first.at[:, pl.ds(1, bx), pl.ds(PAD, by), :], own)
    load.start()
    barrier = pltpu.get_barrier_semaphore()
    for dx in (-1, 0, 1):
        for dy in (-1, 0, 1):
            if dx or dy:
                pl.semaphore_signal(
                    barrier, inc=1, device_id=(ring_x[dx], ring_y[dy]), device_id_type=MESH
                )
    pl.semaphore_wait(barrier, 8)
    load.wait()
    from_x, to_x = {1: bx, -1: 1}, {1: 0, -1: bx + 1}
    from_y, to_y = {1: PAD + by - 1, -1: PAD}, {1: PAD - 1, -1: PAD + by}
    forces = [force[axis] for axis in range(3)]

    def copies(turn):
        plan = [(x_send, x_recv, i, (sign, 0)) for i, sign in enumerate((1, -1))]
        plan += [(y_send, y_recv, i, (0, sign)) for i, sign in enumerate((1, -1))]
        plan += [(c_send, c_recv, i, (dx, dy)) for i, (q, dx, dy) in enumerate(CORNERS)]
        return [
            pltpu.make_async_remote_copy(
                src_ref=source.at[turn, i], dst_ref=goal.at[turn, i],
                send_sem=send.at[turn, k], recv_sem=recv.at[turn, k],
                device_id=(ring_x[dx], ring_y[dy]), device_id_type=MESH,
            )
            for k, (source, goal, i, (dx, dy)) in enumerate(plan)
        ]

    def swap(turn, field):
        for i, sign in enumerate((1, -1)):
            for j, q in enumerate(moving(0, sign)):
                x_send[turn, i, j] = field[q, from_x[sign], PAD : PAD + by, :]

        def gather(x, carry):
            for i, sign in enumerate((1, -1)):
                for j, q in enumerate(moving(1, sign)):
                    y_send[turn, i, j, pl.ds(x, 1), :] = field[
                        q, x + 1, from_y[sign] : from_y[sign] + 1, :
                    ]
            return carry

        lax.fori_loop(0, bx, gather, 0)
        for i, (q, dx, dy) in enumerate(CORNERS):
            c_send[turn, i, 0:1, :] = field[q, from_x[dx], from_y[dy] : from_y[dy] + 1, :]
        moves = copies(turn)
        for move in moves:
            move.start()
        for move in moves:
            move.wait()
        for i, sign in enumerate((1, -1)):
            for j, q in enumerate(moving(0, sign)):
                field[q, to_x[sign], PAD : PAD + by, :] = x_recv[turn, i, j]

        def spread(x, carry):
            for i, sign in enumerate((1, -1)):
                for j, q in enumerate(moving(1, sign)):
                    field[q, x + 1, to_y[sign] : to_y[sign] + 1, :] = y_recv[
                        turn, i, j, pl.ds(x, 1), :
                    ]
            return carry

        lax.fori_loop(0, bx, spread, 0)
        for i, (q, dx, dy) in enumerate(CORNERS):
            field[q, to_x[dx], to_y[dy] : to_y[dy] + 1, :] = c_recv[turn, i, 0:1, :]

    def streamed(field, q, x, h):
        dx, dy, dz = VELOCITY[q]
        window = field[q, x + 1 - dx, PAD + h - dy : PAD + h - dy + 8, :]
        return pltpu.roll(window, dz % LANES, 1) if dz else window

    swap(0, first)

    def middle(x, carry):
        for h in range(0, by, 8):
            dev = [streamed(first, q, x, h) for q in range(19)]
            done = collide(dev, poro[x, h : h + 8], relax[x, h : h + 8], mask[x, h : h + 8], forces)
            for q in range(19):
                second[q, x + 1, PAD + h : PAD + h + 8, :] = done[q]
        return carry

    lax.fori_loop(0, bx, middle, 0)
    swap(1, second)

    def last(x, carry):
        for h in range(0, by, 8):
            for q in range(19):
                out[q, x, h : h + 8, :] = streamed(second, q, x, h)
        return carry

    lax.fori_loop(0, bx, last, 0)


def later_steps(force, post, poro, relax, mask, nx, ny):
    bx, by, nz = poro.shape
    field = pltpu.VMEM((19, bx + 2, by + 2 * PAD, nz), jnp.float32)
    x_face = pltpu.VMEM((2, 2, 5, by, nz), jnp.float32)
    y_face = pltpu.VMEM((2, 2, 5, bx, nz), jnp.float32)
    corner = pltpu.VMEM((2, 4, 8, nz), jnp.float32)
    return pl.pallas_call(
        functools.partial(steps_kernel, nx, ny),
        out_shape=jax.ShapeDtypeStruct((19, bx, by, nz), jnp.float32),
        in_specs=[pl.BlockSpec(memory_space=pltpu.SMEM), pl.BlockSpec(memory_space=pl.ANY)]
        + [pl.BlockSpec(memory_space=pltpu.VMEM)] * 3,
        out_specs=pl.BlockSpec(memory_space=pltpu.VMEM),
        scratch_shapes=[field, field, x_face, y_face, corner, x_face, y_face, corner]
        + [pltpu.SemaphoreType.DMA((2, 8))] * 2
        + [pltpu.SemaphoreType.DMA],
        compiler_params=pltpu.CompilerParams(
            collective_id=1, has_side_effects=True, vmem_limit_bytes=40 * MIB
        ),
        name="stream_steps",
    )(force, post, poro, relax, mask)


def local(pdf_old, tile_target, porosity, relaxation, solid_mask, force):
    nx, ny = lax.axis_size("gx"), lax.axis_size("gy")
    n = nx * ny
    held, _, tile_cells = pdf_old.shape
    capacity = 2 * held // n
    block = solid_mask.shape
    parts = tile_cells // block[2]
    packed, labels = pack(tile_target, jnp.transpose(pdf_old, (1, 0, 2)), n, capacity, parts)
    arrived, places, poro, relax = exchange(packed, labels, porosity, relaxation, nx, ny, block)
    where_to = places[:, :, 0].reshape(n * capacity)
    slots = jnp.arange(n * capacity, dtype=jnp.int32)
    found = where_to[:, None] == jnp.arange(held, dtype=jnp.int32)[None, :]
    slot = jnp.sum(jnp.where(found, slots[:, None], 0), axis=0)
    source, row = slot // capacity, (slot % capacity) * parts
    post = first_collision(
        source, row, force, arrived, poro, relax, solid_mask, capacity, parts
    )
    return later_steps(force, post, poro, relax, solid_mask, nx, ny)


def solution(mesh):
    return jax.shard_map(
        local,
        mesh=mesh,
        in_specs=(
            P(("gx", "gy"), None, None),
            P(("gx", "gy")),
            P(("gx", "gy"), None, None),
            P(("gx", "gy"), None, None),
            P("gx", "gy", None),
            P(),
        ),
        out_specs=P(None, "gx", "gy", None),
        check_vma=False,
    )
```

```python
import functools

import jax
import jax.numpy as jnp
from jax import lax
from jax.experimental import pallas as pl
from jax.experimental.pallas import tpu as pltpu
from jax.sharding import PartitionSpec as P

STEPS = 2
VELOCITY = (
    (0, 0, 0),
    (1, 0, 0),
    (-1, 0, 0),
    (0, 1, 0),
    (0, -1, 0),
    (0, 0, 1),
    (0, 0, -1),
    (1, 1, 0),
    (-1, -1, 0),
    (1, -1, 0),
    (-1, 1, 0),
    (1, 0, 1),
    (-1, 0, -1),
    (1, 0, -1),
    (-1, 0, 1),
    (0, 1, 1),
    (0, -1, -1),
    (0, 1, -1),
    (0, -1, 1),
)
MAGIC = 0.1875
MESH = pl.DeviceIdType.MESH
LANES = 128
PAD = 8
MIB = 1 << 20


def moving(axis, sign):
    return [q for q in range(19) if VELOCITY[q][axis] == sign]


CORNERS = [(q, VELOCITY[q][0], VELOCITY[q][1]) for q in range(19) if VELOCITY[q][0] * VELOCITY[q][1] != 0]


def collide(dev, porosity, omega, mask, force):
    solid = porosity + mask.astype(jnp.float32) * (1.0 - porosity)
    fluid = 1.0 - solid
    omega_minus = (2.0 - omega) / (1.0 + (2.0 * MAGIC - 0.5) * omega)
    sums = {q: dev[q] + dev[q + 1] for q in range(1, 19, 2)}
    gaps = {q: dev[q] - dev[q + 1] for q in range(1, 19, 2)}
    axis_sum = sums[1] + sums[3] + sums[5]
    diagonal_sum = (sums[7] + sums[9]) + (sums[11] + sums[13]) + (sums[15] + sums[17])
    density = dev[0] * (1.0 / 3.0) + axis_sum * (1.0 / 18.0) + diagonal_sum * (1.0 / 36.0)
    flow = []
    for axis in range(3):
        straight = gaps[1 + 2 * axis]
        slanted = None
        for q in range(7, 19, 2):
            if VELOCITY[q][axis]:
                term = gaps[q] if VELOCITY[q][axis] > 0 else -gaps[q]
                slanted = term if slanted is None else slanted + term
        flow.append(straight * (1.0 / 18.0) + slanted * (1.0 / 36.0) + 0.5 * force[axis])
    base = density - 1.5 * (flow[0] * flow[0] + flow[1] * flow[1] + flow[2] * flow[2])
    pull = fluid * omega
    keep = 0.5 * (1.0 - pull)
    turn = 0.5 * (fluid * (1.0 - omega_minus) - solid)
    push = [3.0 * fluid * (omega_minus * flow[axis] + force[axis]) for axis in range(3)]

    def along(vector, velocity):
        total = None
        for axis in range(3):
            if velocity[axis]:
                term = vector[axis] if velocity[axis] > 0 else -vector[axis]
                total = term if total is None else total + term
        return total

    post = [None] * 19
    post[0] = dev[0] + pull * (base - dev[0])
    for q in range(1, 19, 2):
        speed = along(flow, VELOCITY[q])
        even = keep * sums[q] + pull * (base + 4.5 * (speed * speed))
        odd = turn * gaps[q] + along(push, VELOCITY[q])
        post[q] = even + odd
        post[q + 1] = even - odd
    return post


def route_kernel(held, capacity, target, table, labels, count):
    owners = labels.shape[0]
    labels[...] = jnp.full(labels.shape, -1, jnp.int32)

    def clear(d, carry):
        count[d] = 0
        for k in range(capacity):
            table[d * capacity + k] = 0
        return carry

    lax.fori_loop(0, owners, clear, 0)

    def place(k, carry):
        goal = target[k]
        owner = lax.div(goal, held)
        rank = count[owner]
        count[owner] = rank + 1
        table[owner * capacity + rank] = k
        labels[owner, pl.ds(rank, 1), :] = jnp.full((1, LANES), goal - owner * held, jnp.int32)
        return carry

    lax.fori_loop(0, held, place, 0)


def route(target, owners, capacity):
    return pl.pallas_call(
        functools.partial(route_kernel, target.shape[0], capacity),
        out_shape=(
            jax.ShapeDtypeStruct((owners * capacity,), jnp.int32),
            jax.ShapeDtypeStruct((owners, capacity, LANES), jnp.int32),
        ),
        in_specs=[pl.BlockSpec(memory_space=pltpu.SMEM)],
        out_specs=[pl.BlockSpec(memory_space=pltpu.SMEM), pl.BlockSpec(memory_space=pltpu.VMEM)],
        scratch_shapes=[pltpu.SMEM((owners,), jnp.int32)],
        name="route_tiles",
    )(target)


def flow_kernel(nx, ny, capacity, parts,
                table, force, labels, pdf, poro, relax, mask, out,
                halves, packed, arrived, places, slots, slot_of, plane, poro_block, relax_block,
                first, second, x_send, y_send, c_send, x_recv, y_recv, c_recv,
                tile_send, tile_recv, label_send, label_recv, cell_send, cell_recv, own, send, recv):
    n = nx * ny
    held = pdf.shape[1]
    depth = capacity * parts
    a, b = lax.axis_index("gx"), lax.axis_index("gy")
    me = a * ny + b
    bx, by = mask.shape[:2]
    slab = poro.shape[0]
    half = nx // 2
    loads = [
        pltpu.make_async_copy(pdf.at[:, :, pl.ds(r * LANES, LANES)], halves.at[r], own.at[r])
        for r in range(parts)
    ]
    mine = [
        pltpu.make_async_copy(
            whole.at[:, pl.ds(b * by, by), :], block.at[pl.ds(b * slab, slab)], own.at[parts + i]
        )
        for i, (whole, block) in enumerate(((poro, poro_block), (relax, relax_block)))
    ]
    for copy in loads + mine:
        copy.start()

    def partner(o, sign):
        side = 1 - lax.rem(o // (half * ny), 2)
        i = lax.rem(o // ny, half)
        j = lax.rem(o, ny)
        other = lax.rem(a // half + side, 2) * half + lax.rem(lax.rem(a, half) + half + sign * i, half)
        return other, lax.rem(b + ny + sign * j, ny)

    last = n // 2
    order = lambda step: step + lax.div(step, last)
    barrier = pltpu.get_barrier_semaphore()

    def greet(step, carry):
        pl.semaphore_signal(barrier, inc=1, device_id=partner(order(step), 1), device_id_type=MESH)
        return carry

    lax.fori_loop(0, n - 1, greet, 0)
    pl.semaphore_wait(barrier, n - 1)

    def tile_copies(o):
        to, source = partner(o, 1), partner(o, -1)
        goal = to[0] * ny + to[1]
        return (
            pltpu.make_async_remote_copy(
                src_ref=labels.at[goal], dst_ref=places.at[me],
                send_sem=label_send.at[o], recv_sem=label_recv.at[o],
                device_id=to, device_id_type=MESH,
            ),
            pltpu.make_async_remote_copy(
                src_ref=packed.at[goal], dst_ref=arrived.at[me],
                send_sem=tile_send.at[o], recv_sem=tile_recv.at[o],
                device_id=to, device_id_type=MESH,
            ),
        )

    def tile_arrivals(o):
        to, source = partner(o, 1), partner(o, -1)
        origin = source[0] * ny + source[1]
        return (
            pltpu.make_async_remote_copy(
                src_ref=labels.at[origin], dst_ref=places.at[origin],
                send_sem=label_send.at[o], recv_sem=label_recv.at[o],
                device_id=to, device_id_type=MESH,
            ),
            pltpu.make_async_remote_copy(
                src_ref=packed.at[origin], dst_ref=arrived.at[origin],
                send_sem=tile_send.at[o], recv_sem=tile_recv.at[o],
                device_id=to, device_id_type=MESH,
            ),
        )

    def cell_copies(o, source, target):
        return [
            pltpu.make_async_remote_copy(
                src_ref=whole.at[:, pl.ds(target * by, by), :],
                dst_ref=block.at[pl.ds(source * slab, slab)],
                send_sem=cell_send.at[2 * o + i], recv_sem=cell_recv.at[2 * o + i],
                device_id=(a, target), device_id_type=MESH,
            )
            for i, (whole, block) in enumerate(((poro, poro_block), (relax, relax_block)))
        ]

    for copy in loads:
        copy.wait()
    flat = [halves.at[r].reshape(19 * held, LANES) for r in range(parts)]

    def fill(block, goal):
        for k in range(capacity):
            tile = table[goal * capacity + k]
            for r in range(parts):
                block[goal if block is packed else me, pl.ds(k * parts + r, 19, stride=depth), :] = (
                    flat[r][pl.ds(tile, 19, stride=held), :]
                )

    def send_tiles(step, carry):
        o = order(step)
        to = partner(o, 1)
        fill(packed, to[0] * ny + to[1])
        for copy in tile_copies(o):
            copy.start()
        return carry

    lax.fori_loop(0, n - 1, send_tiles, 0)
    for o in range(1, ny):
        for copy in cell_copies(o, b, lax.rem(b + o, ny)):
            copy.start()
    fill(arrived, me)
    places[me] = labels[me]
    for copy in mine:
        copy.wait()
    for o in range(1, ny):
        for copy in cell_copies(o, lax.rem(b + ny - o, ny), lax.rem(b + o, ny)):
            copy.wait_send()
            copy.wait_recv()

    def take_tiles(step, carry):
        for copy in tile_arrivals(order(step)):
            copy.wait_recv()
        return carry

    lax.fori_loop(0, n - 1, take_tiles, 0)

    lane = lax.broadcasted_iota(jnp.int32, (1, LANES), 1)

    def invert(d, total):
        for k in range(capacity):
            total = jnp.maximum(
                total, jnp.where(places[d, k : k + 1, :] == lane, d * capacity + k, 0)
            )
        return total

    slots[...] = lax.fori_loop(0, n, invert, jnp.zeros((1, LANES), jnp.int32))
    down = pltpu.make_async_copy(slots, slot_of, own.at[parts + 2])
    down.start()
    down.wait()
    forces = [force[axis] for axis in range(3)]
    strips = by // parts

    def start(x, carry):
        for j in range(strips):
            slot = slot_of[0, x * strips + j]
            source = lax.div(slot, capacity)
            row = (slot - source * capacity) * parts
            for r in range(parts):
                plane[pl.ds(j * parts + r, 19, stride=by), :] = arrived[
                    source, pl.ds(row + r, 19, stride=depth), :
                ]
        for h in range(0, by, 8):
            dev = [plane[q * by + h : q * by + h + 8, :] for q in range(19)]
            done = collide(
                dev, poro_block[x, h : h + 8], relax_block[x, h : h + 8], mask[x, h : h + 8], forces
            )
            for q in range(19):
                first[q, x + 1, PAD + h : PAD + h + 8, :] = done[q]
        return carry

    lax.fori_loop(0, bx, start, 0)

    ring_x = {1: lax.rem(a + 1, nx), -1: lax.rem(a + nx - 1, nx), 0: a}
    ring_y = {1: lax.rem(b + 1, ny), -1: lax.rem(b + ny - 1, ny), 0: b}
    from_x, to_x = {1: bx, -1: 1}, {1: 0, -1: bx + 1}
    from_y, to_y = {1: PAD + by - 1, -1: PAD}, {1: PAD - 1, -1: PAD + by}

    def copies(turn):
        plan = [(x_send, x_recv, i, (sign, 0)) for i, sign in enumerate((1, -1))]
        plan += [(y_send, y_recv, i, (0, sign)) for i, sign in enumerate((1, -1))]
        plan += [(c_send, c_recv, i, (dx, dy)) for i, (q, dx, dy) in enumerate(CORNERS)]
        return [
            pltpu.make_async_remote_copy(
                src_ref=source.at[turn, i], dst_ref=goal.at[turn, i],
                send_sem=send.at[turn, k], recv_sem=recv.at[turn, k],
                device_id=(ring_x[dx], ring_y[dy]), device_id_type=MESH,
            )
            for k, (source, goal, i, (dx, dy)) in enumerate(plan)
        ]

    def swap(turn, field):
        for i, sign in enumerate((1, -1)):
            for j, q in enumerate(moving(0, sign)):
                x_send[turn, i, j] = field[q, from_x[sign], PAD : PAD + by, :]

        def gather(x, carry):
            for i, sign in enumerate((1, -1)):
                for j, q in enumerate(moving(1, sign)):
                    y_send[turn, i, j, pl.ds(x, 1), :] = field[
                        q, x + 1, from_y[sign] : from_y[sign] + 1, :
                    ]
            return carry

        lax.fori_loop(0, bx, gather, 0)
        for i, (q, dx, dy) in enumerate(CORNERS):
            c_send[turn, i, 0:1, :] = field[q, from_x[dx], from_y[dy] : from_y[dy] + 1, :]
        moves = copies(turn)
        for move in moves:
            move.start()
        for move in moves:
            move.wait()
        for i, sign in enumerate((1, -1)):
            for j, q in enumerate(moving(0, sign)):
                field[q, to_x[sign], PAD : PAD + by, :] = x_recv[turn, i, j]

        def spread(x, carry):
            for i, sign in enumerate((1, -1)):
                for j, q in enumerate(moving(1, sign)):
                    field[q, x + 1, to_y[sign] : to_y[sign] + 1, :] = y_recv[
                        turn, i, j, pl.ds(x, 1), :
                    ]
            return carry

        lax.fori_loop(0, bx, spread, 0)
        for i, (q, dx, dy) in enumerate(CORNERS):
            field[q, to_x[dx], to_y[dy] : to_y[dy] + 1, :] = c_recv[turn, i, 0:1, :]

    def streamed(field, q, x, h):
        dx, dy, dz = VELOCITY[q]
        window = field[q, x + 1 - dx, PAD + h - dy : PAD + h - dy + 8, :]
        return pltpu.roll(window, dz % LANES, 1) if dz else window

    swap(0, first)

    def middle(x, carry):
        for h in range(0, by, 8):
            dev = [streamed(first, q, x, h) for q in range(19)]
            done = collide(
                dev, poro_block[x, h : h + 8], relax_block[x, h : h + 8], mask[x, h : h + 8], forces
            )
            for q in range(19):
                second[q, x + 1, PAD + h : PAD + h + 8, :] = done[q]
        return carry

    lax.fori_loop(0, bx, middle, 0)
    swap(1, second)

    def finish(x, carry):
        for h in range(0, by, 8):
            for q in range(19):
                out[q, x, h : h + 8, :] = streamed(second, q, x, h)
        return carry

    lax.fori_loop(0, bx, finish, 0)

    def sent(step, carry):
        for copy in tile_copies(order(step)):
            copy.wait_send()
        return carry

    lax.fori_loop(0, n - 1, sent, 0)


def local(pdf_old, tile_target, porosity, relaxation, solid_mask, force):
    nx, ny = lax.axis_size("gx"), lax.axis_size("gy")
    n = nx * ny
    held, _, tile_cells = pdf_old.shape
    capacity = 2 * held // n
    bx, by, nz = solid_mask.shape
    parts = tile_cells // nz
    table, labels = route(tile_target, n, capacity)
    tiles = pltpu.VMEM((n, 19 * capacity * parts, nz), jnp.float32)
    block = pltpu.VMEM((bx, by, nz), jnp.float32)
    field = pltpu.VMEM((19, bx + 2, by + 2 * PAD, nz), jnp.float32)
    faces = [
        pltpu.VMEM((2, 2, 5, by, nz), jnp.float32),
        pltpu.VMEM((2, 2, 5, bx, nz), jnp.float32),
        pltpu.VMEM((2, 4, 8, nz), jnp.float32),
    ]
    return pl.pallas_call(
        functools.partial(flow_kernel, nx, ny, capacity, parts),
        out_shape=jax.ShapeDtypeStruct((19, bx, by, nz), jnp.float32),
        in_specs=[pl.BlockSpec(memory_space=pltpu.SMEM)] * 2
        + [pl.BlockSpec(memory_space=pltpu.VMEM)]
        + [pl.BlockSpec(memory_space=pl.ANY)] * 3
        + [pl.BlockSpec(memory_space=pltpu.VMEM)],
        out_specs=pl.BlockSpec(memory_space=pltpu.VMEM),
        scratch_shapes=[
            pltpu.VMEM((parts, 19, held, nz), jnp.float32),
            tiles,
            tiles,
            pltpu.VMEM(labels.shape, jnp.int32),
            pltpu.VMEM((1, LANES), jnp.int32),
            pltpu.SMEM((1, LANES), jnp.int32),
            pltpu.VMEM((19 * by, nz), jnp.float32),
            block,
            block,
            field,
            field,
        ]
        + faces
        + faces
        + [pltpu.SemaphoreType.DMA((n,))] * 4
        + [pltpu.SemaphoreType.DMA((2 * ny,))] * 2
        + [pltpu.SemaphoreType.DMA((parts + 3,))]
        + [pltpu.SemaphoreType.DMA((2, 8))] * 2,
        compiler_params=pltpu.CompilerParams(
            collective_id=0, has_side_effects=True, vmem_limit_bytes=48 * MIB
        ),
        name="exchange_and_flow",
    )(table, force, labels, jnp.transpose(pdf_old, (1, 0, 2)), porosity, relaxation, solid_mask)


def solution(mesh):
    return jax.shard_map(
        local,
        mesh=mesh,
        in_specs=(
            P(("gx", "gy"), None, None),
            P(("gx", "gy")),
            P(("gx", "gy"), None, None),
            P(("gx", "gy"), None, None),
            P("gx", "gy", None),
            P(),
        ),
        out_specs=P(None, "gx", "gy", None),
        check_vma=False,
    )
```

```python
import functools

import jax
import jax.numpy as jnp
from jax import lax
from jax.experimental import pallas as pl
from jax.experimental.pallas import tpu as pltpu
from jax.sharding import PartitionSpec as P

STEPS = 2
VELOCITY = (
    (0, 0, 0),
    (1, 0, 0),
    (-1, 0, 0),
    (0, 1, 0),
    (0, -1, 0),
    (0, 0, 1),
    (0, 0, -1),
    (1, 1, 0),
    (-1, -1, 0),
    (1, -1, 0),
    (-1, 1, 0),
    (1, 0, 1),
    (-1, 0, -1),
    (1, 0, -1),
    (-1, 0, 1),
    (0, 1, 1),
    (0, -1, -1),
    (0, 1, -1),
    (0, -1, 1),
)
MAGIC = 0.1875
MESH = pl.DeviceIdType.MESH
LANES = 128
PAD = 8
MIB = 1 << 20


def moving(axis, sign):
    return [q for q in range(19) if VELOCITY[q][axis] == sign]


CORNERS = [(q, VELOCITY[q][0], VELOCITY[q][1]) for q in range(19) if VELOCITY[q][0] * VELOCITY[q][1] != 0]


def collide(dev, porosity, omega, mask, force):
    solid = porosity + mask.astype(jnp.float32) * (1.0 - porosity)
    fluid = 1.0 - solid
    omega_minus = (2.0 - omega) / (1.0 + (2.0 * MAGIC - 0.5) * omega)
    sums = {q: dev[q] + dev[q + 1] for q in range(1, 19, 2)}
    gaps = {q: dev[q] - dev[q + 1] for q in range(1, 19, 2)}
    axis_sum = sums[1] + sums[3] + sums[5]
    diagonal_sum = (sums[7] + sums[9]) + (sums[11] + sums[13]) + (sums[15] + sums[17])
    density = dev[0] * (1.0 / 3.0) + axis_sum * (1.0 / 18.0) + diagonal_sum * (1.0 / 36.0)
    flow = []
    for axis in range(3):
        straight = gaps[1 + 2 * axis]
        slanted = None
        for q in range(7, 19, 2):
            if VELOCITY[q][axis]:
                term = gaps[q] if VELOCITY[q][axis] > 0 else -gaps[q]
                slanted = term if slanted is None else slanted + term
        flow.append(straight * (1.0 / 18.0) + slanted * (1.0 / 36.0) + 0.5 * force[axis])
    base = density - 1.5 * (flow[0] * flow[0] + flow[1] * flow[1] + flow[2] * flow[2])
    pull = fluid * omega
    keep = 0.5 * (1.0 - pull)
    turn = 0.5 * (fluid * (1.0 - omega_minus) - solid)
    push = [3.0 * fluid * (omega_minus * flow[axis] + force[axis]) for axis in range(3)]

    def along(vector, velocity):
        total = None
        for axis in range(3):
            if velocity[axis]:
                term = vector[axis] if velocity[axis] > 0 else -vector[axis]
                total = term if total is None else total + term
        return total

    post = [None] * 19
    post[0] = dev[0] + pull * (base - dev[0])
    for q in range(1, 19, 2):
        speed = along(flow, VELOCITY[q])
        even = keep * sums[q] + pull * (base + 4.5 * (speed * speed))
        odd = turn * gaps[q] + along(push, VELOCITY[q])
        post[q] = even + odd
        post[q + 1] = even - odd
    return post


def route_kernel(held, capacity, target, table, labels, count):
    owners = labels.shape[0]
    labels[...] = jnp.full(labels.shape, -1, jnp.int32)

    def clear(d, carry):
        count[d] = 0
        for k in range(capacity):
            table[d * capacity + k] = 0
        return carry

    lax.fori_loop(0, owners, clear, 0)

    def place(k, carry):
        goal = target[k]
        owner = lax.div(goal, held)
        rank = count[owner]
        count[owner] = rank + 1
        table[owner * capacity + rank] = k
        labels[owner, pl.ds(rank, 1), :] = jnp.full((1, LANES), goal - owner * held, jnp.int32)
        return carry

    lax.fori_loop(0, held, place, 0)


def route(target, owners, capacity):
    return pl.pallas_call(
        functools.partial(route_kernel, target.shape[0], capacity),
        out_shape=(
            jax.ShapeDtypeStruct((owners * capacity,), jnp.int32),
            jax.ShapeDtypeStruct((owners, capacity, LANES), jnp.int32),
        ),
        in_specs=[pl.BlockSpec(memory_space=pltpu.SMEM)],
        out_specs=[pl.BlockSpec(memory_space=pltpu.SMEM), pl.BlockSpec(memory_space=pltpu.VMEM)],
        scratch_shapes=[pltpu.SMEM((owners,), jnp.int32)],
        name="route_tiles",
    )(target)


def flow_kernel(nx, ny, capacity, parts,
                table, force, labels, pdf, poro, relax, mask, out,
                halves, packed, arrived, places, slots, slot_of, plane, poro_block, relax_block,
                first, second, x_send, y_send, c_send, x_recv, y_recv, c_recv,
                tile_send, tile_recv, label_send, label_recv, cell_send, cell_recv, own, send, recv):
    n = nx * ny
    held = pdf.shape[1]
    depth = capacity * parts
    a, b = lax.axis_index("gx"), lax.axis_index("gy")
    me = a * ny + b
    bx, by = mask.shape[:2]
    slab = poro.shape[0]
    half = nx // 2
    loads = [
        pltpu.make_async_copy(pdf.at[:, :, pl.ds(r * LANES, LANES)], halves.at[r], own.at[r])
        for r in range(parts)
    ]
    mine = [
        pltpu.make_async_copy(
            whole.at[:, pl.ds(b * by, by), :], block.at[pl.ds(b * slab, slab)], own.at[parts + i]
        )
        for i, (whole, block) in enumerate(((poro, poro_block), (relax, relax_block)))
    ]
    for copy in loads + mine:
        copy.start()

    def partner(o, sign):
        side = 1 - lax.rem(o // (half * ny), 2)
        i = lax.rem(o // ny, half)
        j = lax.rem(o, ny)
        other = lax.rem(a // half + side, 2) * half + lax.rem(lax.rem(a, half) + half + sign * i, half)
        return other, lax.rem(b + ny + sign * j, ny)

    def order(step):
        pair = step // 2
        return pair + lax.rem(step, 2) * (n // 2 + 1)

    barrier = pltpu.get_barrier_semaphore()

    def greet(step, carry):
        pl.semaphore_signal(barrier, inc=1, device_id=partner(order(step), 1), device_id_type=MESH)
        return carry

    lax.fori_loop(0, n - 1, greet, 0)
    pl.semaphore_wait(barrier, n - 1)

    def tile_copies(o):
        to, source = partner(o, 1), partner(o, -1)
        goal = to[0] * ny + to[1]
        return (
            pltpu.make_async_remote_copy(
                src_ref=labels.at[goal], dst_ref=places.at[me],
                send_sem=label_send.at[o], recv_sem=label_recv.at[o],
                device_id=to, device_id_type=MESH,
            ),
            pltpu.make_async_remote_copy(
                src_ref=packed.at[goal], dst_ref=arrived.at[me],
                send_sem=tile_send.at[o], recv_sem=tile_recv.at[o],
                device_id=to, device_id_type=MESH,
            ),
        )

    def tile_arrivals(o):
        to, source = partner(o, 1), partner(o, -1)
        origin = source[0] * ny + source[1]
        return (
            pltpu.make_async_remote_copy(
                src_ref=labels.at[origin], dst_ref=places.at[origin],
                send_sem=label_send.at[o], recv_sem=label_recv.at[o],
                device_id=to, device_id_type=MESH,
            ),
            pltpu.make_async_remote_copy(
                src_ref=packed.at[origin], dst_ref=arrived.at[origin],
                send_sem=tile_send.at[o], recv_sem=tile_recv.at[o],
                device_id=to, device_id_type=MESH,
            ),
        )

    def cell_copies(o, source, target):
        return [
            pltpu.make_async_remote_copy(
                src_ref=whole.at[:, pl.ds(target * by, by), :],
                dst_ref=block.at[pl.ds(source * slab, slab)],
                send_sem=cell_send.at[2 * o + i], recv_sem=cell_recv.at[2 * o + i],
                device_id=(a, target), device_id_type=MESH,
            )
            for i, (whole, block) in enumerate(((poro, poro_block), (relax, relax_block)))
        ]

    for copy in loads:
        copy.wait()
    flat = [halves.at[r].reshape(19 * held, LANES) for r in range(parts)]

    def fill(block, goal):
        for k in range(capacity):
            tile = table[goal * capacity + k]
            for r in range(parts):
                block[goal if block is packed else me, pl.ds(k * parts + r, 19, stride=depth), :] = (
                    flat[r][pl.ds(tile, 19, stride=held), :]
                )

    def send_tiles(step, carry):
        o = order(step)
        to = partner(o, 1)
        fill(packed, to[0] * ny + to[1])
        for copy in tile_copies(o):
            copy.start()
        return carry

    lax.fori_loop(0, n - 1, send_tiles, 0)
    for o in range(1, ny):
        for copy in cell_copies(o, b, lax.rem(b + o, ny)):
            copy.start()
    fill(arrived, me)
    places[me] = labels[me]
    for copy in mine:
        copy.wait()
    for o in range(1, ny):
        for copy in cell_copies(o, lax.rem(b + ny - o, ny), lax.rem(b + o, ny)):
            copy.wait_send()
            copy.wait_recv()

    def take_tiles(step, carry):
        for copy in tile_arrivals(order(step)):
            copy.wait_recv()
        return carry

    lax.fori_loop(0, n - 1, take_tiles, 0)

    lane = lax.broadcasted_iota(jnp.int32, (1, LANES), 1)

    def invert(d, total):
        for k in range(capacity):
            total = jnp.maximum(
                total, jnp.where(places[d, k : k + 1, :] == lane, d * capacity + k, 0)
            )
        return total

    slots[...] = lax.fori_loop(0, n, invert, jnp.zeros((1, LANES), jnp.int32))
    down = pltpu.make_async_copy(slots, slot_of, own.at[parts + 2])
    down.start()
    down.wait()
    forces = [force[axis] for axis in range(3)]
    strips = by // parts

    def start(x, carry):
        for j in range(strips):
            slot = slot_of[0, x * strips + j]
            source = lax.div(slot, capacity)
            row = (slot - source * capacity) * parts
            for r in range(parts):
                plane[pl.ds(j * parts + r, 19, stride=by), :] = arrived[
                    source, pl.ds(row + r, 19, stride=depth), :
                ]
        for h in range(0, by, 8):
            dev = [plane[q * by + h : q * by + h + 8, :] for q in range(19)]
            done = collide(
                dev, poro_block[x, h : h + 8], relax_block[x, h : h + 8], mask[x, h : h + 8], forces
            )
            for q in range(19):
                first[q, x + 1, PAD + h : PAD + h + 8, :] = done[q]
        return carry

    lax.fori_loop(0, bx, start, 0)

    ring_x = {1: lax.rem(a + 1, nx), -1: lax.rem(a + nx - 1, nx), 0: a}
    ring_y = {1: lax.rem(b + 1, ny), -1: lax.rem(b + ny - 1, ny), 0: b}
    from_x, to_x = {1: bx, -1: 1}, {1: 0, -1: bx + 1}
    from_y, to_y = {1: PAD + by - 1, -1: PAD}, {1: PAD - 1, -1: PAD + by}

    def copies(turn):
        plan = [(x_send, x_recv, i, (sign, 0)) for i, sign in enumerate((1, -1))]
        plan += [(y_send, y_recv, i, (0, sign)) for i, sign in enumerate((1, -1))]
        plan += [(c_send, c_recv, i, (dx, dy)) for i, (q, dx, dy) in enumerate(CORNERS)]
        return [
            pltpu.make_async_remote_copy(
                src_ref=source.at[turn, i], dst_ref=goal.at[turn, i],
                send_sem=send.at[turn, k], recv_sem=recv.at[turn, k],
                device_id=(ring_x[dx], ring_y[dy]), device_id_type=MESH,
            )
            for k, (source, goal, i, (dx, dy)) in enumerate(plan)
        ]

    def swap(turn, field):
        for i, sign in enumerate((1, -1)):
            for j, q in enumerate(moving(0, sign)):
                x_send[turn, i, j] = field[q, from_x[sign], PAD : PAD + by, :]

        def gather(x, carry):
            for i, sign in enumerate((1, -1)):
                for j, q in enumerate(moving(1, sign)):
                    y_send[turn, i, j, pl.ds(x, 1), :] = field[
                        q, x + 1, from_y[sign] : from_y[sign] + 1, :
                    ]
            return carry

        lax.fori_loop(0, bx, gather, 0)
        for i, (q, dx, dy) in enumerate(CORNERS):
            c_send[turn, i, 0:1, :] = field[q, from_x[dx], from_y[dy] : from_y[dy] + 1, :]
        moves = copies(turn)
        for move in moves:
            move.start()
        for move in moves:
            move.wait()
        for i, sign in enumerate((1, -1)):
            for j, q in enumerate(moving(0, sign)):
                field[q, to_x[sign], PAD : PAD + by, :] = x_recv[turn, i, j]

        def spread(x, carry):
            for i, sign in enumerate((1, -1)):
                for j, q in enumerate(moving(1, sign)):
                    field[q, x + 1, to_y[sign] : to_y[sign] + 1, :] = y_recv[
                        turn, i, j, pl.ds(x, 1), :
                    ]
            return carry

        lax.fori_loop(0, bx, spread, 0)
        for i, (q, dx, dy) in enumerate(CORNERS):
            field[q, to_x[dx], to_y[dy] : to_y[dy] + 1, :] = c_recv[turn, i, 0:1, :]

    def streamed(field, q, x, h):
        dx, dy, dz = VELOCITY[q]
        window = field[q, x + 1 - dx, PAD + h - dy : PAD + h - dy + 8, :]
        return pltpu.roll(window, dz % LANES, 1) if dz else window

    swap(0, first)

    def middle(x, carry):
        for h in range(0, by, 8):
            dev = [streamed(first, q, x, h) for q in range(19)]
            done = collide(
                dev, poro_block[x, h : h + 8], relax_block[x, h : h + 8], mask[x, h : h + 8], forces
            )
            for q in range(19):
                second[q, x + 1, PAD + h : PAD + h + 8, :] = done[q]
        return carry

    lax.fori_loop(0, bx, middle, 0)
    swap(1, second)

    def finish(x, carry):
        for h in range(0, by, 8):
            for q in range(19):
                out[q, x, h : h + 8, :] = streamed(second, q, x, h)
        return carry

    lax.fori_loop(0, bx, finish, 0)

    def sent(step, carry):
        for copy in tile_copies(order(step)):
            copy.wait_send()
        return carry

    lax.fori_loop(0, n - 1, sent, 0)


def local(pdf_old, tile_target, porosity, relaxation, solid_mask, force):
    nx, ny = lax.axis_size("gx"), lax.axis_size("gy")
    n = nx * ny
    held, _, tile_cells = pdf_old.shape
    capacity = 2 * held // n
    bx, by, nz = solid_mask.shape
    parts = tile_cells // nz
    table, labels = route(tile_target, n, capacity)
    tiles = pltpu.VMEM((n, 19 * capacity * parts, nz), jnp.float32)
    block = pltpu.VMEM((bx, by, nz), jnp.float32)
    field = pltpu.VMEM((19, bx + 2, by + 2 * PAD, nz), jnp.float32)
    faces = [
        pltpu.VMEM((2, 2, 5, by, nz), jnp.float32),
        pltpu.VMEM((2, 2, 5, bx, nz), jnp.float32),
        pltpu.VMEM((2, 4, 8, nz), jnp.float32),
    ]
    return pl.pallas_call(
        functools.partial(flow_kernel, nx, ny, capacity, parts),
        out_shape=jax.ShapeDtypeStruct((19, bx, by, nz), jnp.float32),
        in_specs=[pl.BlockSpec(memory_space=pltpu.SMEM)] * 2
        + [pl.BlockSpec(memory_space=pltpu.VMEM)]
        + [pl.BlockSpec(memory_space=pl.ANY)] * 3
        + [pl.BlockSpec(memory_space=pltpu.VMEM)],
        out_specs=pl.BlockSpec(memory_space=pltpu.VMEM),
        scratch_shapes=[
            pltpu.VMEM((parts, 19, held, nz), jnp.float32),
            tiles,
            tiles,
            pltpu.VMEM(labels.shape, jnp.int32),
            pltpu.VMEM((1, LANES), jnp.int32),
            pltpu.SMEM((1, LANES), jnp.int32),
            pltpu.VMEM((19 * by, nz), jnp.float32),
            block,
            block,
            field,
            field,
        ]
        + faces
        + faces
        + [pltpu.SemaphoreType.DMA((n,))] * 4
        + [pltpu.SemaphoreType.DMA((2 * ny,))] * 2
        + [pltpu.SemaphoreType.DMA((parts + 3,))]
        + [pltpu.SemaphoreType.DMA((2, 8))] * 2,
        compiler_params=pltpu.CompilerParams(
            collective_id=0, has_side_effects=True, vmem_limit_bytes=62 * MIB
        ),
        name="exchange_and_flow",
    )(table, force, labels, jnp.transpose(pdf_old, (1, 0, 2)), porosity, relaxation, solid_mask)


def solution(mesh):
    return jax.shard_map(
        local,
        mesh=mesh,
        in_specs=(
            P(("gx", "gy"), None, None),
            P(("gx", "gy")),
            P(("gx", "gy"), None, None),
            P(("gx", "gy"), None, None),
            P("gx", "gy", None),
            P(),
        ),
        out_specs=P(None, "gx", "gy", None),
        check_vma=False,
    )
```

```python
import functools

import jax
import jax.numpy as jnp
from jax import lax
from jax.experimental import pallas as pl
from jax.experimental.pallas import tpu as pltpu
from jax.sharding import PartitionSpec as P

STEPS = 2
VELOCITY = (
    (0, 0, 0),
    (1, 0, 0),
    (-1, 0, 0),
    (0, 1, 0),
    (0, -1, 0),
    (0, 0, 1),
    (0, 0, -1),
    (1, 1, 0),
    (-1, -1, 0),
    (1, -1, 0),
    (-1, 1, 0),
    (1, 0, 1),
    (-1, 0, -1),
    (1, 0, -1),
    (-1, 0, 1),
    (0, 1, 1),
    (0, -1, -1),
    (0, 1, -1),
    (0, -1, 1),
)
MAGIC = 0.1875
MESH = pl.DeviceIdType.MESH
LANES = 128
PAD = 8
MIB = 1 << 20


def moving(axis, sign):
    return [q for q in range(19) if VELOCITY[q][axis] == sign]


CORNERS = [(q, VELOCITY[q][0], VELOCITY[q][1]) for q in range(19) if VELOCITY[q][0] * VELOCITY[q][1] != 0]


def collide(dev, porosity, omega, mask, force):
    solid = porosity + mask.astype(jnp.float32) * (1.0 - porosity)
    fluid = 1.0 - solid
    omega_minus = (2.0 - omega) / (1.0 + (2.0 * MAGIC - 0.5) * omega)
    sums = {q: dev[q] + dev[q + 1] for q in range(1, 19, 2)}
    gaps = {q: dev[q] - dev[q + 1] for q in range(1, 19, 2)}
    axis_sum = sums[1] + sums[3] + sums[5]
    diagonal_sum = (sums[7] + sums[9]) + (sums[11] + sums[13]) + (sums[15] + sums[17])
    density = dev[0] * (1.0 / 3.0) + axis_sum * (1.0 / 18.0) + diagonal_sum * (1.0 / 36.0)
    flow = []
    for axis in range(3):
        straight = gaps[1 + 2 * axis]
        slanted = None
        for q in range(7, 19, 2):
            if VELOCITY[q][axis]:
                term = gaps[q] if VELOCITY[q][axis] > 0 else -gaps[q]
                slanted = term if slanted is None else slanted + term
        flow.append(straight * (1.0 / 18.0) + slanted * (1.0 / 36.0) + 0.5 * force[axis])
    base = density - 1.5 * (flow[0] * flow[0] + flow[1] * flow[1] + flow[2] * flow[2])
    pull = fluid * omega
    keep = 0.5 * (1.0 - pull)
    turn = 0.5 * (fluid * (1.0 - omega_minus) - solid)
    push = [3.0 * fluid * (omega_minus * flow[axis] + force[axis]) for axis in range(3)]

    def along(vector, velocity):
        total = None
        for axis in range(3):
            if velocity[axis]:
                term = vector[axis] if velocity[axis] > 0 else -vector[axis]
                total = term if total is None else total + term
        return total

    post = [None] * 19
    post[0] = dev[0] + pull * (base - dev[0])
    for q in range(1, 19, 2):
        speed = along(flow, VELOCITY[q])
        even = keep * sums[q] + pull * (base + 4.5 * (speed * speed))
        odd = turn * gaps[q] + along(push, VELOCITY[q])
        post[q] = even + odd
        post[q + 1] = even - odd
    return post


def column(rows, diagonal):
    return jnp.sum(jnp.where(diagonal, rows, 0), axis=1, keepdims=True)


def fill_tables(held, capacity, goal, table, labels):
    sub = lax.broadcasted_iota(jnp.int32, (held, LANES), 0)
    lane = lax.broadcasted_iota(jnp.int32, (held, LANES), 1)
    diagonal = sub == lane
    goals = jnp.broadcast_to(goal[...], (held, LANES))
    owners = lax.shift_right_logical(goals, held.bit_length() - 1)
    inner = goals - owners * held
    same = (column(owners, diagonal) == owners) & (sub < lane)
    rank = jnp.sum(jnp.where(same, 1, 0), axis=0, keepdims=True)
    slot = column(owners * capacity + rank, diagonal)
    place = column(inner, diagonal)
    for c in range(table.shape[0]):
        hit = slot == lane + c * LANES
        table[c : c + 1, :] = jnp.max(jnp.where(hit, sub, 0), axis=0, keepdims=True)
        labels[c : c + 1, :] = jnp.max(jnp.where(hit, place, -1), axis=0, keepdims=True)


def flow_kernel(nx, ny, capacity, parts,
                force, goal, pdf, poro, relax, mask_hbm, out,
                table_rows, table, labels, gathered, mask, halves, packed, arrived, places, slots,
                slot_of, plane, poro_block, relax_block,
                first, second, x_send, y_send, c_send, x_recv, y_recv, c_recv,
                tile_send, tile_recv, label_send, label_recv, cell_send, cell_recv, own, send, recv):
    n = nx * ny
    held = pdf.shape[1]
    depth = capacity * parts
    a, b = lax.axis_index("gx"), lax.axis_index("gy")
    me = a * ny + b
    bx, by = mask.shape[:2]
    slab = poro.shape[0]
    half = nx // 2
    loads = [
        pltpu.make_async_copy(pdf.at[:, :, pl.ds(r * LANES, LANES)], halves.at[r], own.at[r])
        for r in range(parts)
    ]
    mine = [
        pltpu.make_async_copy(
            whole.at[:, pl.ds(b * by, by), :], block.at[pl.ds(b * slab, slab)], own.at[parts + i]
        )
        for i, (whole, block) in enumerate(((poro, poro_block), (relax, relax_block)))
    ]
    mine.append(pltpu.make_async_copy(mask_hbm, mask, own.at[parts + 2]))
    down = pltpu.make_async_copy(table_rows, table, own.at[parts + 3])
    for copy in loads + mine:
        copy.start()

    def partner(o, sign):
        side = 1 - lax.rem(o // (half * ny), 2)
        i = lax.rem(o // ny, half)
        j = lax.rem(o, ny)
        other = lax.rem(a // half + side, 2) * half + lax.rem(lax.rem(a, half) + half + sign * i, half)
        return other, lax.rem(b + ny + sign * j, ny)

    def order(step):
        pair = step // 2
        return pair + lax.rem(step, 2) * (n // 2 + 1)

    barrier = pltpu.get_barrier_semaphore()

    def greet(step, carry):
        pl.semaphore_signal(barrier, inc=1, device_id=partner(order(step), 1), device_id_type=MESH)
        return carry

    lax.fori_loop(0, n - 1, greet, 0)
    fill_tables(held, capacity, goal, table_rows, labels)
    down.start()
    down.wait()
    pl.semaphore_wait(barrier, n - 1)

    def tile_copies(o):
        to, source = partner(o, 1), partner(o, -1)
        goal = to[0] * ny + to[1]
        return (
            pltpu.make_async_remote_copy(
                src_ref=labels, dst_ref=places.at[me],
                send_sem=label_send.at[o], recv_sem=label_recv.at[o],
                device_id=to, device_id_type=MESH,
            ),
            pltpu.make_async_remote_copy(
                src_ref=packed.at[goal], dst_ref=arrived.at[me],
                send_sem=tile_send.at[o], recv_sem=tile_recv.at[o],
                device_id=to, device_id_type=MESH,
            ),
        )

    def tile_arrivals(o):
        to, source = partner(o, 1), partner(o, -1)
        origin = source[0] * ny + source[1]
        return (
            pltpu.make_async_remote_copy(
                src_ref=labels, dst_ref=places.at[origin],
                send_sem=label_send.at[o], recv_sem=label_recv.at[o],
                device_id=to, device_id_type=MESH,
            ),
            pltpu.make_async_remote_copy(
                src_ref=packed.at[origin], dst_ref=arrived.at[origin],
                send_sem=tile_send.at[o], recv_sem=tile_recv.at[o],
                device_id=to, device_id_type=MESH,
            ),
        )

    def cell_copies(o, source, target):
        return [
            pltpu.make_async_remote_copy(
                src_ref=whole.at[:, pl.ds(target * by, by), :],
                dst_ref=block.at[pl.ds(source * slab, slab)],
                send_sem=cell_send.at[2 * o + i], recv_sem=cell_recv.at[2 * o + i],
                device_id=(a, target), device_id_type=MESH,
            )
            for i, (whole, block) in enumerate(((poro, poro_block), (relax, relax_block)))
        ]

    for copy in loads:
        copy.wait()
    flat = [halves.at[r].reshape(19 * held, LANES) for r in range(parts)]

    def fill(block, goal):
        for k in range(capacity):
            spot = goal * capacity + k
            tile = table[spot // LANES, lax.rem(spot, LANES)]
            for r in range(parts):
                block[goal if block is packed else me, pl.ds(k * parts + r, 19, stride=depth), :] = (
                    flat[r][pl.ds(tile, 19, stride=held), :]
                )

    def send_tiles(step, carry):
        o = order(step)
        to = partner(o, 1)
        fill(packed, to[0] * ny + to[1])
        for copy in tile_copies(o):
            copy.start()
        return carry

    lax.fori_loop(0, n - 1, send_tiles, 0)
    for o in range(1, ny):
        for copy in cell_copies(o, b, lax.rem(b + o, ny)):
            copy.start()
    fill(arrived, me)
    places[me] = labels[...]
    for copy in mine:
        copy.wait()
    for o in range(1, ny):
        for copy in cell_copies(o, lax.rem(b + ny - o, ny), lax.rem(b + o, ny)):
            copy.wait_send()
            copy.wait_recv()

    def take_tiles(step, carry):
        for copy in tile_arrivals(order(step)):
            copy.wait_recv()
        return carry

    lax.fori_loop(0, n - 1, take_tiles, 0)

    chunk, offset = (me * capacity) // LANES, lax.rem(me * capacity, LANES)

    def collect(d, carry):
        gathered[pl.ds(d, 1), :] = places[d, pl.ds(chunk, 1), :]
        return carry

    lax.fori_loop(0, n, collect, 0)
    rows = gathered[...]
    sender = lax.broadcasted_iota(jnp.int32, (n, LANES), 0)
    lane = lax.broadcasted_iota(jnp.int32, (n, LANES), 1)
    found = jnp.zeros((n, LANES), jnp.int32)
    for k in range(capacity):
        label = jnp.sum(jnp.where(lane == offset + k, rows, 0), axis=1, keepdims=True)
        found = jnp.maximum(found, jnp.where(label == lane, sender * capacity + k, 0))
    slots[...] = jnp.max(found, axis=0, keepdims=True)
    lift = pltpu.make_async_copy(slots, slot_of, own.at[parts + 4])
    lift.start()
    lift.wait()
    forces = [force[axis] for axis in range(3)]
    strips = by // parts

    def start(x, carry):
        for j in range(strips):
            slot = slot_of[0, x * strips + j]
            source = lax.div(slot, capacity)
            row = (slot - source * capacity) * parts
            for r in range(parts):
                plane[pl.ds(j * parts + r, 19, stride=by), :] = arrived[
                    source, pl.ds(row + r, 19, stride=depth), :
                ]
        for h in range(0, by, 8):
            dev = [plane[q * by + h : q * by + h + 8, :] for q in range(19)]
            done = collide(
                dev, poro_block[x, h : h + 8], relax_block[x, h : h + 8], mask[x, h : h + 8], forces
            )
            for q in range(19):
                first[q, x + 1, PAD + h : PAD + h + 8, :] = done[q]
        return carry

    lax.fori_loop(0, bx, start, 0)

    ring_x = {1: lax.rem(a + 1, nx), -1: lax.rem(a + nx - 1, nx), 0: a}
    ring_y = {1: lax.rem(b + 1, ny), -1: lax.rem(b + ny - 1, ny), 0: b}
    from_x, to_x = {1: bx, -1: 1}, {1: 0, -1: bx + 1}
    from_y, to_y = {1: PAD + by - 1, -1: PAD}, {1: PAD - 1, -1: PAD + by}

    def copies(turn):
        plan = [(x_send, x_recv, i, (sign, 0)) for i, sign in enumerate((1, -1))]
        plan += [(y_send, y_recv, i, (0, sign)) for i, sign in enumerate((1, -1))]
        plan += [(c_send, c_recv, i, (dx, dy)) for i, (q, dx, dy) in enumerate(CORNERS)]
        return [
            pltpu.make_async_remote_copy(
                src_ref=source.at[turn, i], dst_ref=goal.at[turn, i],
                send_sem=send.at[turn, k], recv_sem=recv.at[turn, k],
                device_id=(ring_x[dx], ring_y[dy]), device_id_type=MESH,
            )
            for k, (source, goal, i, (dx, dy)) in enumerate(plan)
        ]

    def swap(turn, field):
        for i, sign in enumerate((1, -1)):
            for j, q in enumerate(moving(0, sign)):
                x_send[turn, i, j] = field[q, from_x[sign], PAD : PAD + by, :]

        def gather(x, carry):
            for i, sign in enumerate((1, -1)):
                for j, q in enumerate(moving(1, sign)):
                    y_send[turn, i, j, pl.ds(x, 1), :] = field[
                        q, x + 1, from_y[sign] : from_y[sign] + 1, :
                    ]
            return carry

        lax.fori_loop(0, bx, gather, 0)
        for i, (q, dx, dy) in enumerate(CORNERS):
            c_send[turn, i, 0:1, :] = field[q, from_x[dx], from_y[dy] : from_y[dy] + 1, :]
        moves = copies(turn)
        for move in moves:
            move.start()
        for move in moves:
            move.wait()
        for i, sign in enumerate((1, -1)):
            for j, q in enumerate(moving(0, sign)):
                field[q, to_x[sign], PAD : PAD + by, :] = x_recv[turn, i, j]

        def spread(x, carry):
            for i, sign in enumerate((1, -1)):
                for j, q in enumerate(moving(1, sign)):
                    field[q, x + 1, to_y[sign] : to_y[sign] + 1, :] = y_recv[
                        turn, i, j, pl.ds(x, 1), :
                    ]
            return carry

        lax.fori_loop(0, bx, spread, 0)
        for i, (q, dx, dy) in enumerate(CORNERS):
            field[q, to_x[dx], to_y[dy] : to_y[dy] + 1, :] = c_recv[turn, i, 0:1, :]

    def streamed(field, q, x, h):
        dx, dy, dz = VELOCITY[q]
        window = field[q, x + 1 - dx, PAD + h - dy : PAD + h - dy + 8, :]
        return pltpu.roll(window, dz % LANES, 1) if dz else window

    swap(0, first)

    def middle(x, carry):
        for h in range(0, by, 8):
            dev = [streamed(first, q, x, h) for q in range(19)]
            done = collide(
                dev, poro_block[x, h : h + 8], relax_block[x, h : h + 8], mask[x, h : h + 8], forces
            )
            for q in range(19):
                second[q, x + 1, PAD + h : PAD + h + 8, :] = done[q]
        return carry

    lax.fori_loop(0, bx, middle, 0)
    swap(1, second)

    def finish(x, carry):
        for h in range(0, by, 8):
            for q in range(19):
                out[q, x, h : h + 8, :] = streamed(second, q, x, h)
        return carry

    lax.fori_loop(0, bx, finish, 0)

    def sent(step, carry):
        for copy in tile_copies(order(step)):
            copy.wait_send()
        return carry

    lax.fori_loop(0, n - 1, sent, 0)


def local(pdf_old, tile_target, porosity, relaxation, solid_mask, force):
    nx, ny = lax.axis_size("gx"), lax.axis_size("gy")
    n = nx * ny
    held, _, tile_cells = pdf_old.shape
    capacity = 2 * held // n
    bx, by, nz = solid_mask.shape
    parts = tile_cells // nz
    chunks = n * capacity // LANES
    tiles = pltpu.VMEM((n, 19 * capacity * parts, nz), jnp.float32)
    block = pltpu.VMEM((bx, by, nz), jnp.float32)
    field = pltpu.VMEM((19, bx + 2, by + 2 * PAD, nz), jnp.float32)
    faces = [
        pltpu.VMEM((2, 2, 5, by, nz), jnp.float32),
        pltpu.VMEM((2, 2, 5, bx, nz), jnp.float32),
        pltpu.VMEM((2, 4, 8, nz), jnp.float32),
    ]
    return pl.pallas_call(
        functools.partial(flow_kernel, nx, ny, capacity, parts),
        out_shape=jax.ShapeDtypeStruct((19, bx, by, nz), jnp.float32),
        in_specs=[pl.BlockSpec(memory_space=pltpu.SMEM), pl.BlockSpec(memory_space=pltpu.VMEM)]
        + [pl.BlockSpec(memory_space=pl.ANY)] * 4,
        out_specs=pl.BlockSpec(memory_space=pltpu.VMEM),
        scratch_shapes=[
            pltpu.VMEM((chunks, LANES), jnp.int32),
            pltpu.SMEM((chunks, LANES), jnp.int32),
            pltpu.VMEM((chunks, LANES), jnp.int32),
            pltpu.VMEM((n, LANES), jnp.int32),
            pltpu.VMEM((bx, by, nz), jnp.int32),
            pltpu.VMEM((parts, 19, held, nz), jnp.float32),
            tiles,
            tiles,
            pltpu.VMEM((n, chunks, LANES), jnp.int32),
            pltpu.VMEM((1, LANES), jnp.int32),
            pltpu.SMEM((1, LANES), jnp.int32),
            pltpu.VMEM((19 * by, nz), jnp.float32),
            block,
            block,
            field,
            field,
        ]
        + faces
        + faces
        + [pltpu.SemaphoreType.DMA((n,))] * 4
        + [pltpu.SemaphoreType.DMA((2 * ny,))] * 2
        + [pltpu.SemaphoreType.DMA((parts + 5,))]
        + [pltpu.SemaphoreType.DMA((2, 8))] * 2,
        compiler_params=pltpu.CompilerParams(
            collective_id=0, has_side_effects=True, vmem_limit_bytes=62 * MIB
        ),
        name="exchange_and_flow",
    )(
        force,
        tile_target.reshape(1, held),
        jnp.transpose(pdf_old, (1, 0, 2)),
        porosity,
        relaxation,
        solid_mask,
    )


def solution(mesh):
    return jax.shard_map(
        local,
        mesh=mesh,
        in_specs=(
            P(("gx", "gy"), None, None),
            P(("gx", "gy")),
            P(("gx", "gy"), None, None),
            P(("gx", "gy"), None, None),
            P("gx", "gy", None),
            P(),
        ),
        out_specs=P(None, "gx", "gy", None),
        check_vma=False,
    )
```

```python
import functools

import jax
import jax.numpy as jnp
from jax import lax
from jax.experimental import pallas as pl
from jax.experimental.pallas import tpu as pltpu
from jax.sharding import PartitionSpec as P

STEPS = 2
VELOCITY = (
    (0, 0, 0),
    (1, 0, 0),
    (-1, 0, 0),
    (0, 1, 0),
    (0, -1, 0),
    (0, 0, 1),
    (0, 0, -1),
    (1, 1, 0),
    (-1, -1, 0),
    (1, -1, 0),
    (-1, 1, 0),
    (1, 0, 1),
    (-1, 0, -1),
    (1, 0, -1),
    (-1, 0, 1),
    (0, 1, 1),
    (0, -1, -1),
    (0, 1, -1),
    (0, -1, 1),
)
MAGIC = 0.1875
MESH = pl.DeviceIdType.MESH
LANES = 128
PAD = 8
MIB = 1 << 20


def moving(axis, sign):
    return [q for q in range(19) if VELOCITY[q][axis] == sign]


CORNERS = [(q, VELOCITY[q][0], VELOCITY[q][1]) for q in range(19) if VELOCITY[q][0] * VELOCITY[q][1] != 0]


def collide(dev, porosity, omega, mask, force):
    solid = porosity + mask.astype(jnp.float32) * (1.0 - porosity)
    fluid = 1.0 - solid
    omega_minus = (2.0 - omega) / (1.0 + (2.0 * MAGIC - 0.5) * omega)
    sums = {q: dev[q] + dev[q + 1] for q in range(1, 19, 2)}
    gaps = {q: dev[q] - dev[q + 1] for q in range(1, 19, 2)}
    axis_sum = sums[1] + sums[3] + sums[5]
    diagonal_sum = (sums[7] + sums[9]) + (sums[11] + sums[13]) + (sums[15] + sums[17])
    density = dev[0] * (1.0 / 3.0) + axis_sum * (1.0 / 18.0) + diagonal_sum * (1.0 / 36.0)
    flow = []
    for axis in range(3):
        straight = gaps[1 + 2 * axis]
        slanted = None
        for q in range(7, 19, 2):
            if VELOCITY[q][axis]:
                term = gaps[q] if VELOCITY[q][axis] > 0 else -gaps[q]
                slanted = term if slanted is None else slanted + term
        flow.append(straight * (1.0 / 18.0) + slanted * (1.0 / 36.0) + 0.5 * force[axis])
    base = density - 1.5 * (flow[0] * flow[0] + flow[1] * flow[1] + flow[2] * flow[2])
    pull = fluid * omega
    keep = 0.5 * (1.0 - pull)
    turn = 0.5 * (fluid * (1.0 - omega_minus) - solid)
    push = [3.0 * fluid * (omega_minus * flow[axis] + force[axis]) for axis in range(3)]

    def along(vector, velocity):
        total = None
        for axis in range(3):
            if velocity[axis]:
                term = vector[axis] if velocity[axis] > 0 else -vector[axis]
                total = term if total is None else total + term
        return total

    post = [None] * 19
    post[0] = dev[0] + pull * (base - dev[0])
    for q in range(1, 19, 2):
        speed = along(flow, VELOCITY[q])
        even = keep * sums[q] + pull * (base + 4.5 * (speed * speed))
        odd = turn * gaps[q] + along(push, VELOCITY[q])
        post[q] = even + odd
        post[q + 1] = even - odd
    return post


def column(rows, diagonal):
    return jnp.sum(jnp.where(diagonal, rows, 0), axis=1, keepdims=True)


def fill_tables(held, capacity, goal, table, labels):
    sub = lax.broadcasted_iota(jnp.int32, (held, LANES), 0)
    lane = lax.broadcasted_iota(jnp.int32, (held, LANES), 1)
    diagonal = sub == lane
    goals = jnp.broadcast_to(goal[...], (held, LANES))
    owners = lax.shift_right_logical(goals, held.bit_length() - 1)
    inner = goals - owners * held
    same = (column(owners, diagonal) == owners) & (sub < lane)
    rank = jnp.sum(jnp.where(same, 1, 0), axis=0, keepdims=True)
    slot = column(owners * capacity + rank, diagonal)
    place = column(inner, diagonal)
    for c in range(table.shape[0]):
        hit = slot == lane + c * LANES
        table[c : c + 1, :] = jnp.max(jnp.where(hit, sub, 0), axis=0, keepdims=True)
        labels[c : c + 1, :] = jnp.max(jnp.where(hit, place, -1), axis=0, keepdims=True)


def reach(bx, by):
    return {1: 0, -1: bx + 1}, {1: PAD - 1, -1: PAD + by}


def unpack_faces(field, x_face, y_face, c_face, bx, by):
    to_x, to_y = reach(bx, by)
    for i, sign in enumerate((1, -1)):
        for j, q in enumerate(moving(0, sign)):
            field[q, to_x[sign], PAD : PAD + by, :] = x_face[i, j]

    def spread(x, carry):
        for i, sign in enumerate((1, -1)):
            for j, q in enumerate(moving(1, sign)):
                field[q, x + 1, to_y[sign] : to_y[sign] + 1, :] = y_face[i, j, pl.ds(x, 1), :]
        return carry

    lax.fori_loop(0, bx, spread, 0)
    for i, (q, dx, dy) in enumerate(CORNERS):
        field[q, to_x[dx], to_y[dy] : to_y[dy] + 1, :] = c_face[i, 0:1, :]


def streamed(field, q, x, h):
    dx, dy, dz = VELOCITY[q]
    window = field[q, x + 1 - dx, PAD + h - dy : PAD + h - dy + 8, :]
    return pltpu.roll(window, dz % LANES, 1) if dz else window


def finish_kernel(pieces, middle, x_face, y_face, c_face, out, field, stage, x_in, y_in, c_in,
                  load_sem, store_sem, face_sem):
    bx, by = out.shape[1:3]
    size = bx // pieces
    loads = [
        pltpu.make_async_copy(
            middle.at[:, pl.ds(c * size, size)],
            field.at[:, pl.ds(1 + c * size, size), pl.ds(PAD, by), :],
            load_sem.at[c],
        )
        for c in range(pieces)
    ]
    stores = [
        pltpu.make_async_copy(
            stage.at[:, pl.ds(c * size, size)], out.at[:, pl.ds(c * size, size)], store_sem.at[c]
        )
        for c in range(pieces)
    ]
    faces = [
        pltpu.make_async_copy(face, ref, face_sem.at[i])
        for i, (face, ref) in enumerate(((x_face, x_in), (y_face, y_in), (c_face, c_in)))
    ]
    for copy in faces + loads:
        copy.start()
    for copy in faces:
        copy.wait()
    unpack_faces(field, x_in, y_in, c_in, bx, by)
    loads[0].wait()

    def plane(x, carry):
        for h in range(0, by, 8):
            for q in range(19):
                stage[q, x, h : h + 8, :] = streamed(field, q, x, h)
        return carry

    for c in range(pieces):
        if c + 1 < pieces:
            loads[c + 1].wait()
        lax.fori_loop(c * size, (c + 1) * size, plane, 0)
        stores[c].start()
    for store in stores:
        store.wait()


def flow_kernel(nx, ny, capacity, parts,
                force, goal, pdf, poro, relax, mask_hbm, middle, x_out, y_out, c_out,
                table_rows, table, labels, gathered, mask, halves, packed, arrived, places, slots,
                slot_of, plane, poro_block, relax_block,
                first, second, x_send, y_send, c_send, x_recv, y_recv, c_recv,
                tile_send, tile_recv, label_send, label_recv, cell_send, cell_recv, own, send, recv):
    n = nx * ny
    held = pdf.shape[1]
    depth = capacity * parts
    a, b = lax.axis_index("gx"), lax.axis_index("gy")
    me = a * ny + b
    bx, by = mask.shape[:2]
    slab = poro.shape[0]
    half = nx // 2
    loads = [
        pltpu.make_async_copy(pdf.at[:, :, pl.ds(r * LANES, LANES)], halves.at[r], own.at[r])
        for r in range(parts)
    ]
    mine = [
        pltpu.make_async_copy(
            whole.at[:, pl.ds(b * by, by), :], block.at[pl.ds(b * slab, slab)], own.at[parts + i]
        )
        for i, (whole, block) in enumerate(((poro, poro_block), (relax, relax_block)))
    ]
    mine.append(pltpu.make_async_copy(mask_hbm, mask, own.at[parts + 2]))
    down = pltpu.make_async_copy(table_rows, table, own.at[parts + 3])
    for copy in loads + mine:
        copy.start()

    def partner(o, sign):
        side = 1 - lax.rem(o // (half * ny), 2)
        i = lax.rem(o // ny, half)
        j = lax.rem(o, ny)
        other = lax.rem(a // half + side, 2) * half + lax.rem(lax.rem(a, half) + half + sign * i, half)
        return other, lax.rem(b + ny + sign * j, ny)

    def order(step):
        pair = step // 2
        return pair + lax.rem(step, 2) * (n // 2 + 1)

    barrier = pltpu.get_barrier_semaphore()

    def greet(step, carry):
        pl.semaphore_signal(barrier, inc=1, device_id=partner(order(step), 1), device_id_type=MESH)
        return carry

    lax.fori_loop(0, n - 1, greet, 0)
    fill_tables(held, capacity, goal, table_rows, labels)
    down.start()
    down.wait()
    pl.semaphore_wait(barrier, n - 1)

    def tile_copies(o):
        to, source = partner(o, 1), partner(o, -1)
        goal = to[0] * ny + to[1]
        return (
            pltpu.make_async_remote_copy(
                src_ref=labels, dst_ref=places.at[me],
                send_sem=label_send.at[o], recv_sem=label_recv.at[o],
                device_id=to, device_id_type=MESH,
            ),
            pltpu.make_async_remote_copy(
                src_ref=packed.at[goal], dst_ref=arrived.at[me],
                send_sem=tile_send.at[o], recv_sem=tile_recv.at[o],
                device_id=to, device_id_type=MESH,
            ),
        )

    def tile_arrivals(o):
        to, source = partner(o, 1), partner(o, -1)
        origin = source[0] * ny + source[1]
        return (
            pltpu.make_async_remote_copy(
                src_ref=labels, dst_ref=places.at[origin],
                send_sem=label_send.at[o], recv_sem=label_recv.at[o],
                device_id=to, device_id_type=MESH,
            ),
            pltpu.make_async_remote_copy(
                src_ref=packed.at[origin], dst_ref=arrived.at[origin],
                send_sem=tile_send.at[o], recv_sem=tile_recv.at[o],
                device_id=to, device_id_type=MESH,
            ),
        )

    def cell_copies(o, source, target):
        return [
            pltpu.make_async_remote_copy(
                src_ref=whole.at[:, pl.ds(target * by, by), :],
                dst_ref=block.at[pl.ds(source * slab, slab)],
                send_sem=cell_send.at[2 * o + i], recv_sem=cell_recv.at[2 * o + i],
                device_id=(a, target), device_id_type=MESH,
            )
            for i, (whole, block) in enumerate(((poro, poro_block), (relax, relax_block)))
        ]

    for copy in loads:
        copy.wait()
    flat = [halves.at[r].reshape(19 * held, LANES) for r in range(parts)]

    def fill(block, goal):
        for k in range(capacity):
            spot = goal * capacity + k
            tile = table[spot // LANES, lax.rem(spot, LANES)]
            for r in range(parts):
                block[goal if block is packed else me, pl.ds(k * parts + r, 19, stride=depth), :] = (
                    flat[r][pl.ds(tile, 19, stride=held), :]
                )

    def send_tiles(step, carry):
        o = order(step)
        to = partner(o, 1)
        fill(packed, to[0] * ny + to[1])
        for copy in tile_copies(o):
            copy.start()
        return carry

    lax.fori_loop(0, n - 1, send_tiles, 0)
    for o in range(1, ny):
        for copy in cell_copies(o, b, lax.rem(b + o, ny)):
            copy.start()
    fill(arrived, me)
    places[me] = labels[...]
    for copy in mine:
        copy.wait()
    for o in range(1, ny):
        for copy in cell_copies(o, lax.rem(b + ny - o, ny), lax.rem(b + o, ny)):
            copy.wait_send()
            copy.wait_recv()

    def take_tiles(step, carry):
        for copy in tile_arrivals(order(step)):
            copy.wait_recv()
        return carry

    lax.fori_loop(0, n - 1, take_tiles, 0)

    chunk, offset = (me * capacity) // LANES, lax.rem(me * capacity, LANES)

    def collect(d, carry):
        gathered[pl.ds(d, 1), :] = places[d, pl.ds(chunk, 1), :]
        return carry

    lax.fori_loop(0, n, collect, 0)
    rows = gathered[...]
    sender = lax.broadcasted_iota(jnp.int32, (n, LANES), 0)
    lane = lax.broadcasted_iota(jnp.int32, (n, LANES), 1)
    found = jnp.zeros((n, LANES), jnp.int32)
    for k in range(capacity):
        label = jnp.sum(jnp.where(lane == offset + k, rows, 0), axis=1, keepdims=True)
        found = jnp.maximum(found, jnp.where(label == lane, sender * capacity + k, 0))
    slots[...] = jnp.max(found, axis=0, keepdims=True)
    lift = pltpu.make_async_copy(slots, slot_of, own.at[parts + 4])
    lift.start()
    lift.wait()
    forces = [force[axis] for axis in range(3)]
    strips = by // parts

    def start(x, carry):
        for j in range(strips):
            slot = slot_of[0, x * strips + j]
            source = lax.div(slot, capacity)
            row = (slot - source * capacity) * parts
            for r in range(parts):
                plane[pl.ds(j * parts + r, 19, stride=by), :] = arrived[
                    source, pl.ds(row + r, 19, stride=depth), :
                ]
        for h in range(0, by, 8):
            dev = [plane[q * by + h : q * by + h + 8, :] for q in range(19)]
            done = collide(
                dev, poro_block[x, h : h + 8], relax_block[x, h : h + 8], mask[x, h : h + 8], forces
            )
            for q in range(19):
                first[q, x + 1, PAD + h : PAD + h + 8, :] = done[q]
        return carry

    lax.fori_loop(0, bx, start, 0)

    ring_x = {1: lax.rem(a + 1, nx), -1: lax.rem(a + nx - 1, nx), 0: a}
    ring_y = {1: lax.rem(b + 1, ny), -1: lax.rem(b + ny - 1, ny), 0: b}
    from_x, from_y = {1: bx, -1: 1}, {1: PAD + by - 1, -1: PAD}

    def copies(turn):
        plan = [(x_send, x_recv, i, (sign, 0)) for i, sign in enumerate((1, -1))]
        plan += [(y_send, y_recv, i, (0, sign)) for i, sign in enumerate((1, -1))]
        plan += [(c_send, c_recv, i, (dx, dy)) for i, (q, dx, dy) in enumerate(CORNERS)]
        return [
            pltpu.make_async_remote_copy(
                src_ref=source.at[turn, i], dst_ref=goal.at[turn, i],
                send_sem=send.at[turn, k], recv_sem=recv.at[turn, k],
                device_id=(ring_x[dx], ring_y[dy]), device_id_type=MESH,
            )
            for k, (source, goal, i, (dx, dy)) in enumerate(plan)
        ]

    def send_faces(turn, field):
        for i, sign in enumerate((1, -1)):
            for j, q in enumerate(moving(0, sign)):
                x_send[turn, i, j] = field[q, from_x[sign], PAD : PAD + by, :]

        def gather(x, carry):
            for i, sign in enumerate((1, -1)):
                for j, q in enumerate(moving(1, sign)):
                    y_send[turn, i, j, pl.ds(x, 1), :] = field[
                        q, x + 1, from_y[sign] : from_y[sign] + 1, :
                    ]
            return carry

        lax.fori_loop(0, bx, gather, 0)
        for i, (q, dx, dy) in enumerate(CORNERS):
            c_send[turn, i, 0:1, :] = field[q, from_x[dx], from_y[dy] : from_y[dy] + 1, :]
        for move in copies(turn):
            move.start()

    def take_faces(turn, field):
        for move in copies(turn):
            move.wait()
        unpack_faces(field, x_recv.at[turn], y_recv.at[turn], c_recv.at[turn], bx, by)

    def block(x, h):
        dev = [streamed(first, q, x, h) for q in range(19)]
        done = collide(
            dev, poro_block[x, h : h + 8], relax_block[x, h : h + 8], mask[x, h : h + 8], forces
        )
        for q in range(19):
            second[q, x + 1, PAD + h : PAD + h + 8, :] = done[q]

    def second_step(x, carry):
        for h in range(0, by, 8):
            block(x, h)
        return carry

    tall = by + 2 * PAD
    first_rows = first.reshape(19 * (bx + 2) * tall, LANES)
    second_rows = second.reshape(19 * (bx + 2) * tall, LANES)
    cell_rows = [ref.reshape(bx * by, LANES) for ref in (poro_block, relax_block, mask)]

    def edge(row, x):
        dev = []
        for q in range(19):
            dx, dy, dz = VELOCITY[q]
            begin = (q * (bx + 2) + x + 1 - dx) * tall + PAD + row - dy
            window = first_rows[pl.ds(begin, 8, stride=tall), :]
            dev.append(pltpu.roll(window, dz % LANES, 1) if dz else window)
        cells = [ref[pl.ds(x * by + row, 8, stride=by), :] for ref in cell_rows]
        done = collide(dev, *cells, forces)
        for q in range(19):
            begin = (q * (bx + 2) + x + 1) * tall + PAD + row
            second_rows[pl.ds(begin, 8, stride=tall), :] = done[q]

    send_faces(0, first)
    lax.fori_loop(1, bx - 1, second_step, 0)
    take_faces(0, first)
    for x in (0, bx - 1):
        second_step(x, 0)
    for x in range(0, bx, 8):
        for row in (0, by - 1):
            edge(row, x)
    keep = pltpu.make_async_copy(
        second.at[:, pl.ds(1, bx), pl.ds(PAD, by), :], middle, own.at[0]
    )
    keep.start()
    send_faces(1, second)
    for move in copies(1):
        move.wait()
    faces = [
        pltpu.make_async_copy(ref.at[1], face, own.at[1 + i])
        for i, (ref, face) in enumerate(((x_recv, x_out), (y_recv, y_out), (c_recv, c_out)))
    ]
    for copy in faces:
        copy.start()
    for copy in faces:
        copy.wait()
    keep.wait()

    def sent(step, carry):
        for copy in tile_copies(order(step)):
            copy.wait_send()
        return carry

    lax.fori_loop(0, n - 1, sent, 0)


def local(pdf_old, tile_target, porosity, relaxation, solid_mask, force):
    nx, ny = lax.axis_size("gx"), lax.axis_size("gy")
    n = nx * ny
    held, _, tile_cells = pdf_old.shape
    capacity = 2 * held // n
    bx, by, nz = solid_mask.shape
    parts = tile_cells // nz
    chunks = n * capacity // LANES
    tiles = pltpu.VMEM((n, 19 * capacity * parts, nz), jnp.float32)
    block = pltpu.VMEM((bx, by, nz), jnp.float32)
    field = pltpu.VMEM((19, bx + 2, by + 2 * PAD, nz), jnp.float32)
    faces = [
        pltpu.VMEM((2, 2, 5, by, nz), jnp.float32),
        pltpu.VMEM((2, 2, 5, bx, nz), jnp.float32),
        pltpu.VMEM((2, 4, 8, nz), jnp.float32),
    ]
    result = jax.ShapeDtypeStruct((19, bx, by, nz), jnp.float32)
    slim = [(2, 5, by, nz), (2, 5, bx, nz), (4, 8, nz)]
    halos = [jax.ShapeDtypeStruct(shape, jnp.float32) for shape in slim]
    middle = pl.pallas_call(
        functools.partial(flow_kernel, nx, ny, capacity, parts),
        out_shape=[result] + halos,
        in_specs=[pl.BlockSpec(memory_space=pltpu.SMEM), pl.BlockSpec(memory_space=pltpu.VMEM)]
        + [pl.BlockSpec(memory_space=pl.ANY)] * 4,
        out_specs=[pl.BlockSpec(memory_space=pl.ANY)] * 4,
        scratch_shapes=[
            pltpu.VMEM((chunks, LANES), jnp.int32),
            pltpu.SMEM((chunks, LANES), jnp.int32),
            pltpu.VMEM((chunks, LANES), jnp.int32),
            pltpu.VMEM((n, LANES), jnp.int32),
            pltpu.VMEM((bx, by, nz), jnp.int32),
            pltpu.VMEM((parts, 19, held, nz), jnp.float32),
            tiles,
            tiles,
            pltpu.VMEM((n, chunks, LANES), jnp.int32),
            pltpu.VMEM((1, LANES), jnp.int32),
            pltpu.SMEM((1, LANES), jnp.int32),
            pltpu.VMEM((19 * by, nz), jnp.float32),
            block,
            block,
            field,
            field,
        ]
        + faces
        + faces
        + [pltpu.SemaphoreType.DMA((n,))] * 4
        + [pltpu.SemaphoreType.DMA((2 * ny,))] * 2
        + [pltpu.SemaphoreType.DMA((parts + 5,))]
        + [pltpu.SemaphoreType.DMA((2, 8))] * 2,
        compiler_params=pltpu.CompilerParams(
            collective_id=0, has_side_effects=True, vmem_limit_bytes=62 * MIB
        ),
        name="exchange_and_flow",
    )(
        force,
        tile_target.reshape(1, held),
        jnp.transpose(pdf_old, (1, 0, 2)),
        porosity,
        relaxation,
        solid_mask,
    )
    pieces = 4
    return pl.pallas_call(
        functools.partial(finish_kernel, pieces),
        out_shape=result,
        in_specs=[pl.BlockSpec(memory_space=pl.ANY)] * 4,
        out_specs=pl.BlockSpec(memory_space=pl.ANY),
        scratch_shapes=[field, pltpu.VMEM((19, bx, by, nz), jnp.float32)]
        + [pltpu.VMEM(shape, jnp.float32) for shape in slim]
        + [pltpu.SemaphoreType.DMA((pieces,))] * 2
        + [pltpu.SemaphoreType.DMA((3,))],
        compiler_params=pltpu.CompilerParams(vmem_limit_bytes=62 * MIB),
        name="last_stream",
    )(*middle)


def solution(mesh):
    return jax.shard_map(
        local,
        mesh=mesh,
        in_specs=(
            P(("gx", "gy"), None, None),
            P(("gx", "gy")),
            P(("gx", "gy"), None, None),
            P(("gx", "gy"), None, None),
            P("gx", "gy", None),
            P(),
        ),
        out_specs=P(None, "gx", "gy", None),
        check_vma=False,
    )
```

```python
import functools

import jax
import jax.numpy as jnp
from jax import lax
from jax.experimental import pallas as pl
from jax.experimental.pallas import tpu as pltpu
from jax.sharding import PartitionSpec as P

STEPS = 2
VELOCITY = (
    (0, 0, 0),
    (1, 0, 0),
    (-1, 0, 0),
    (0, 1, 0),
    (0, -1, 0),
    (0, 0, 1),
    (0, 0, -1),
    (1, 1, 0),
    (-1, -1, 0),
    (1, -1, 0),
    (-1, 1, 0),
    (1, 0, 1),
    (-1, 0, -1),
    (1, 0, -1),
    (-1, 0, 1),
    (0, 1, 1),
    (0, -1, -1),
    (0, 1, -1),
    (0, -1, 1),
)
MAGIC = 0.1875
MESH = pl.DeviceIdType.MESH
LANES = 128
PAD = 8
MIB = 1 << 20


def moving(axis, sign):
    return [q for q in range(19) if VELOCITY[q][axis] == sign]


CORNERS = [(q, VELOCITY[q][0], VELOCITY[q][1]) for q in range(19) if VELOCITY[q][0] * VELOCITY[q][1] != 0]


def collide(dev, porosity, omega, mask, force):
    solid = porosity + mask.astype(jnp.float32) * (1.0 - porosity)
    fluid = 1.0 - solid
    omega_minus = (2.0 - omega) / (1.0 + (2.0 * MAGIC - 0.5) * omega)
    sums = {q: dev[q] + dev[q + 1] for q in range(1, 19, 2)}
    gaps = {q: dev[q] - dev[q + 1] for q in range(1, 19, 2)}
    axis_sum = sums[1] + sums[3] + sums[5]
    diagonal_sum = (sums[7] + sums[9]) + (sums[11] + sums[13]) + (sums[15] + sums[17])
    density = dev[0] * (1.0 / 3.0) + axis_sum * (1.0 / 18.0) + diagonal_sum * (1.0 / 36.0)
    flow = []
    for axis in range(3):
        straight = gaps[1 + 2 * axis]
        slanted = None
        for q in range(7, 19, 2):
            if VELOCITY[q][axis]:
                term = gaps[q] if VELOCITY[q][axis] > 0 else -gaps[q]
                slanted = term if slanted is None else slanted + term
        flow.append(straight * (1.0 / 18.0) + slanted * (1.0 / 36.0) + 0.5 * force[axis])
    base = density - 1.5 * (flow[0] * flow[0] + flow[1] * flow[1] + flow[2] * flow[2])
    pull = fluid * omega
    keep = 0.5 * (1.0 - pull)
    turn = 0.5 * (fluid * (1.0 - omega_minus) - solid)
    push = [3.0 * fluid * (omega_minus * flow[axis] + force[axis]) for axis in range(3)]

    def along(vector, velocity):
        total = None
        for axis in range(3):
            if velocity[axis]:
                term = vector[axis] if velocity[axis] > 0 else -vector[axis]
                total = term if total is None else total + term
        return total

    post = [None] * 19
    post[0] = dev[0] + pull * (base - dev[0])
    for q in range(1, 19, 2):
        speed = along(flow, VELOCITY[q])
        even = keep * sums[q] + pull * (base + 4.5 * (speed * speed))
        odd = turn * gaps[q] + along(push, VELOCITY[q])
        post[q] = even + odd
        post[q + 1] = even - odd
    return post


def column(rows, diagonal):
    return jnp.sum(jnp.where(diagonal, rows, 0), axis=1, keepdims=True)


def fill_tables(held, capacity, goal, table, labels):
    sub = lax.broadcasted_iota(jnp.int32, (held, LANES), 0)
    lane = lax.broadcasted_iota(jnp.int32, (held, LANES), 1)
    diagonal = sub == lane
    goals = jnp.broadcast_to(goal[...], (held, LANES))
    owners = lax.shift_right_logical(goals, held.bit_length() - 1)
    inner = goals - owners * held
    same = (column(owners, diagonal) == owners) & (sub < lane)
    rank = jnp.sum(jnp.where(same, 1, 0), axis=0, keepdims=True)
    slot = column(owners * capacity + rank, diagonal)
    place = column(inner, diagonal)
    for c in range(table.shape[0]):
        hit = slot == lane + c * LANES
        table[c : c + 1, :] = jnp.max(jnp.where(hit, sub, 0), axis=0, keepdims=True)
        labels[c : c + 1, :] = jnp.max(jnp.where(hit, place, -1), axis=0, keepdims=True)


def reach(bx, by):
    return {1: 0, -1: bx + 1}, {1: PAD - 1, -1: PAD + by}


def unpack_faces(field, x_face, y_face, c_face, bx, by):
    to_x, to_y = reach(bx, by)
    for i, sign in enumerate((1, -1)):
        for j, q in enumerate(moving(0, sign)):
            field[q, to_x[sign], PAD : PAD + by, :] = x_face[i, j]

    def spread(x, carry):
        for i, sign in enumerate((1, -1)):
            for j, q in enumerate(moving(1, sign)):
                field[q, x + 1, to_y[sign] : to_y[sign] + 1, :] = y_face[i, j, pl.ds(x, 1), :]
        return carry

    lax.fori_loop(0, bx, spread, 0)
    for i, (q, dx, dy) in enumerate(CORNERS):
        field[q, to_x[dx], to_y[dy] : to_y[dy] + 1, :] = c_face[i, 0:1, :]


def streamed(field, q, x, h):
    dx, dy, dz = VELOCITY[q]
    window = field[q, x + 1 - dx, PAD + h - dy : PAD + h - dy + 8, :]
    return pltpu.roll(window, dz % LANES, 1) if dz else window


def finish_kernel(pieces, middle, x_face, y_face, c_face, out, field, stage, x_in, y_in, c_in,
                  load_sem, store_sem, face_sem):
    bx, by = out.shape[1:3]
    size = bx // pieces
    loads = [
        pltpu.make_async_copy(
            middle.at[:, pl.ds(c * size, size)],
            field.at[:, pl.ds(1 + c * size, size), pl.ds(PAD, by), :],
            load_sem.at[c],
        )
        for c in range(pieces)
    ]
    stores = [
        pltpu.make_async_copy(
            stage.at[:, pl.ds(c * size, size)], out.at[:, pl.ds(c * size, size)], store_sem.at[c]
        )
        for c in range(pieces)
    ]
    faces = [
        pltpu.make_async_copy(face, ref, face_sem.at[i])
        for i, (face, ref) in enumerate(((x_face, x_in), (y_face, y_in), (c_face, c_in)))
    ]
    for copy in faces + loads:
        copy.start()
    for copy in faces:
        copy.wait()
    unpack_faces(field, x_in, y_in, c_in, bx, by)
    loads[0].wait()

    def plane(x, carry):
        for h in range(0, by, 8):
            for q in range(19):
                stage[q, x, h : h + 8, :] = streamed(field, q, x, h)
        return carry

    for c in range(pieces):
        if c + 1 < pieces:
            loads[c + 1].wait()
        lax.fori_loop(c * size, (c + 1) * size, plane, 0)
        stores[c].start()
    for store in stores:
        store.wait()


def flow_kernel(nx, ny, capacity, parts,
                force, goal, pdf, poro, relax, mask_hbm, middle, x_out, y_out, c_out,
                table_rows, table, labels, gathered, mask, halves, packed, arrived, places, slots,
                slot_of, label_of, near_poro, near_relax, near_mask, poro_block, relax_block,
                first, second, x_send, y_send, c_send, x_recv, y_recv, c_recv,
                tile_send, tile_recv, label_send, label_recv, cell_send, cell_recv, own, send, recv):
    n = nx * ny
    held = pdf.shape[1]
    depth = capacity * parts
    a, b = lax.axis_index("gx"), lax.axis_index("gy")
    me = a * ny + b
    bx, by = mask.shape[:2]
    slab = poro.shape[0]
    half = nx // 2
    loads = [
        pltpu.make_async_copy(pdf.at[:, :, pl.ds(r * LANES, LANES)], halves.at[r], own.at[r])
        for r in range(parts)
    ]
    mine = [
        pltpu.make_async_copy(
            whole.at[:, pl.ds(b * by, by), :], block.at[pl.ds(b * slab, slab)], own.at[parts + i]
        )
        for i, (whole, block) in enumerate(((poro, poro_block), (relax, relax_block)))
    ]
    mine.append(pltpu.make_async_copy(mask_hbm, mask, own.at[parts + 2]))
    down = pltpu.make_async_copy(table_rows, table, own.at[parts + 3])
    for copy in loads + mine:
        copy.start()

    def partner(o, sign):
        side = 1 - lax.rem(o // (half * ny), 2)
        i = lax.rem(o // ny, half)
        j = lax.rem(o, ny)
        other = lax.rem(a // half + side, 2) * half + lax.rem(lax.rem(a, half) + half + sign * i, half)
        return other, lax.rem(b + ny + sign * j, ny)

    def order(step):
        pair = step // 2
        return pair + lax.rem(step, 2) * (n // 2 + 1)

    barrier = pltpu.get_barrier_semaphore()

    def greet(step, carry):
        pl.semaphore_signal(barrier, inc=1, device_id=partner(order(step), 1), device_id_type=MESH)
        return carry

    lax.fori_loop(0, n - 1, greet, 0)
    fill_tables(held, capacity, goal, table_rows, labels)
    down.start()
    down.wait()
    pl.semaphore_wait(barrier, n - 1)

    def label_copy(o, slot):
        return pltpu.make_async_remote_copy(
            src_ref=labels, dst_ref=places.at[slot],
            send_sem=label_send.at[o], recv_sem=label_recv.at[o],
            device_id=partner(o, 1), device_id_type=MESH,
        )

    def tile_copy(o, source, slot):
        return pltpu.make_async_remote_copy(
            src_ref=packed.at[source], dst_ref=arrived.at[slot],
            send_sem=tile_send.at[o], recv_sem=tile_recv.at[o],
            device_id=partner(o, 1), device_id_type=MESH,
        )

    def number(device):
        return device[0] * ny + device[1]

    def cell_copies(o, source, target):
        return [
            pltpu.make_async_remote_copy(
                src_ref=whole.at[:, pl.ds(target * by, by), :],
                dst_ref=block.at[pl.ds(source * slab, slab)],
                send_sem=cell_send.at[2 * o + i], recv_sem=cell_recv.at[2 * o + i],
                device_id=(a, target), device_id_type=MESH,
            )
            for i, (whole, block) in enumerate(((poro, poro_block), (relax, relax_block)))
        ]

    for copy in loads:
        copy.wait()
    flat = [halves.at[r].reshape(19 * held, LANES) for r in range(parts)]

    def fill(block, goal):
        for k in range(capacity):
            spot = goal * capacity + k
            tile = table[spot // LANES, lax.rem(spot, LANES)]
            for r in range(parts):
                block[goal if block is packed else me, pl.ds(k * parts + r, 19, stride=depth), :] = (
                    flat[r][pl.ds(tile, 19, stride=held), :]
                )

    def send_tiles(step, carry):
        o = order(step)
        goal_device = number(partner(o, 1))
        fill(packed, goal_device)
        tile_copy(o, goal_device, me).start()
        return carry

    def send_labels(step, carry):
        label_copy(order(step), me).start()
        return carry

    lax.fori_loop(0, n - 1, send_labels, 0)
    lax.fori_loop(0, n - 1, send_tiles, 0)
    for o in range(1, ny):
        for copy in cell_copies(o, b, lax.rem(b + o, ny)):
            copy.start()
    fill(arrived, me)
    places[me] = labels[...]
    for copy in mine:
        copy.wait()
    for o in range(1, ny):
        for copy in cell_copies(o, lax.rem(b + ny - o, ny), lax.rem(b + o, ny)):
            copy.wait_send()
            copy.wait_recv()

    def take_labels(step, carry):
        o = order(step)
        label_copy(o, number(partner(o, -1))).wait_recv()
        return carry

    lax.fori_loop(0, n - 1, take_labels, 0)
    chunk, offset = (me * capacity) // LANES, lax.rem(me * capacity, LANES)

    def collect(d, carry):
        gathered[pl.ds(d, 1), :] = places[d, pl.ds(chunk, 1), :]
        return carry

    lax.fori_loop(0, n, collect, 0)
    rows = gathered[...]
    sender = lax.broadcasted_iota(jnp.int32, (n, LANES), 0)
    lane = lax.broadcasted_iota(jnp.int32, (n, LANES), 1)
    found = jnp.zeros((n, LANES), jnp.int32)
    for k in range(capacity):
        label = jnp.sum(jnp.where(lane == offset + k, rows, 0), axis=1, keepdims=True)
        found = jnp.maximum(found, jnp.where(label == lane, sender * capacity + k, 0))
    slots[...] = jnp.max(found, axis=0, keepdims=True)
    lift = pltpu.make_async_copy(slots, slot_of, own.at[parts + 4])
    spread_out = pltpu.make_async_copy(gathered, label_of, own.at[parts + 5])
    lift.start()
    spread_out.start()
    lift.wait()
    spread_out.wait()
    forces = [force[axis] for axis in range(3)]
    strips = by // parts
    cell_rows = [ref.reshape(bx * by, LANES) for ref in (poro_block, relax_block, mask)]
    size = min(8, depth)

    def collide_block(source):
        for k in range(capacity):
            begin = jnp.maximum(label_of[source, offset + k], 0) * parts
            for rows_of, near in zip(cell_rows, (near_poro, near_relax, near_mask)):
                near[k * parts : (k + 1) * parts, :] = rows_of[pl.ds(begin, parts), :]
        for h in range(0, depth, size):
            dev = [arrived[source, q * depth + h : q * depth + h + size, :] for q in range(19)]
            near = [ref[h : h + size, :] for ref in (near_poro, near_relax, near_mask)]
            done = collide(dev, *near, forces)
            for q in range(19):
                arrived[source, q * depth + h : q * depth + h + size, :] = done[q]

    collide_block(me)

    def take_tiles(step, carry):
        o = order(step)
        source = number(partner(o, -1))
        tile_copy(o, source, source).wait_recv()
        collide_block(source)
        return carry

    lax.fori_loop(0, n - 1, take_tiles, 0)
    tall = by + 2 * PAD
    first_rows = first.reshape(19 * (bx + 2) * tall, LANES)

    def start(x, carry):
        for j in range(strips):
            slot = slot_of[0, x * strips + j]
            source = lax.div(slot, capacity)
            row = (slot - source * capacity) * parts
            for r in range(parts):
                begin = (x + 1) * tall + PAD + j * parts + r
                first_rows[pl.ds(begin, 19, stride=(bx + 2) * tall), :] = arrived[
                    source, pl.ds(row + r, 19, stride=depth), :
                ]
        return carry

    lax.fori_loop(0, bx, start, 0)

    ring_x = {1: lax.rem(a + 1, nx), -1: lax.rem(a + nx - 1, nx), 0: a}
    ring_y = {1: lax.rem(b + 1, ny), -1: lax.rem(b + ny - 1, ny), 0: b}
    from_x, from_y = {1: bx, -1: 1}, {1: PAD + by - 1, -1: PAD}

    def copies(turn):
        plan = [(x_send, x_recv, i, (sign, 0)) for i, sign in enumerate((1, -1))]
        plan += [(y_send, y_recv, i, (0, sign)) for i, sign in enumerate((1, -1))]
        plan += [(c_send, c_recv, i, (dx, dy)) for i, (q, dx, dy) in enumerate(CORNERS)]
        return [
            pltpu.make_async_remote_copy(
                src_ref=source.at[turn, i], dst_ref=goal.at[turn, i],
                send_sem=send.at[turn, k], recv_sem=recv.at[turn, k],
                device_id=(ring_x[dx], ring_y[dy]), device_id_type=MESH,
            )
            for k, (source, goal, i, (dx, dy)) in enumerate(plan)
        ]

    def send_faces(turn, field):
        for i, sign in enumerate((1, -1)):
            for j, q in enumerate(moving(0, sign)):
                x_send[turn, i, j] = field[q, from_x[sign], PAD : PAD + by, :]

        def gather(x, carry):
            for i, sign in enumerate((1, -1)):
                for j, q in enumerate(moving(1, sign)):
                    y_send[turn, i, j, pl.ds(x, 1), :] = field[
                        q, x + 1, from_y[sign] : from_y[sign] + 1, :
                    ]
            return carry

        lax.fori_loop(0, bx, gather, 0)
        for i, (q, dx, dy) in enumerate(CORNERS):
            c_send[turn, i, 0:1, :] = field[q, from_x[dx], from_y[dy] : from_y[dy] + 1, :]
        for move in copies(turn):
            move.start()

    def take_faces(turn, field):
        for move in copies(turn):
            move.wait()
        unpack_faces(field, x_recv.at[turn], y_recv.at[turn], c_recv.at[turn], bx, by)

    def block(x, h):
        dev = [streamed(first, q, x, h) for q in range(19)]
        done = collide(
            dev, poro_block[x, h : h + 8], relax_block[x, h : h + 8], mask[x, h : h + 8], forces
        )
        for q in range(19):
            second[q, x + 1, PAD + h : PAD + h + 8, :] = done[q]

    def second_step(x, carry):
        for h in range(0, by, 8):
            block(x, h)
        return carry

    second_rows = second.reshape(19 * (bx + 2) * tall, LANES)

    def edge(row, x):
        dev = []
        for q in range(19):
            dx, dy, dz = VELOCITY[q]
            begin = (q * (bx + 2) + x + 1 - dx) * tall + PAD + row - dy
            window = first_rows[pl.ds(begin, 8, stride=tall), :]
            dev.append(pltpu.roll(window, dz % LANES, 1) if dz else window)
        cells = [ref[pl.ds(x * by + row, 8, stride=by), :] for ref in cell_rows]
        done = collide(dev, *cells, forces)
        for q in range(19):
            begin = (q * (bx + 2) + x + 1) * tall + PAD + row
            second_rows[pl.ds(begin, 8, stride=tall), :] = done[q]

    send_faces(0, first)
    lax.fori_loop(1, bx - 1, second_step, 0)
    take_faces(0, first)
    for x in (0, bx - 1):
        second_step(x, 0)
    for x in range(0, bx, 8):
        for row in (0, by - 1):
            edge(row, x)
    keep = pltpu.make_async_copy(
        second.at[:, pl.ds(1, bx), pl.ds(PAD, by), :], middle, own.at[0]
    )
    keep.start()
    send_faces(1, second)
    for move in copies(1):
        move.wait()
    faces = [
        pltpu.make_async_copy(ref.at[1], face, own.at[1 + i])
        for i, (ref, face) in enumerate(((x_recv, x_out), (y_recv, y_out), (c_recv, c_out)))
    ]
    for copy in faces:
        copy.start()
    for copy in faces:
        copy.wait()
    keep.wait()

    def sent(step, carry):
        o = order(step)
        label_copy(o, me).wait_send()
        tile_copy(o, number(partner(o, 1)), me).wait_send()
        return carry

    lax.fori_loop(0, n - 1, sent, 0)


def local(pdf_old, tile_target, porosity, relaxation, solid_mask, force):
    nx, ny = lax.axis_size("gx"), lax.axis_size("gy")
    n = nx * ny
    held, _, tile_cells = pdf_old.shape
    capacity = 2 * held // n
    bx, by, nz = solid_mask.shape
    parts = tile_cells // nz
    chunks = n * capacity // LANES
    tiles = pltpu.VMEM((n, 19 * capacity * parts, nz), jnp.float32)
    block = pltpu.VMEM((bx, by, nz), jnp.float32)
    field = pltpu.VMEM((19, bx + 2, by + 2 * PAD, nz), jnp.float32)
    faces = [
        pltpu.VMEM((2, 2, 5, by, nz), jnp.float32),
        pltpu.VMEM((2, 2, 5, bx, nz), jnp.float32),
        pltpu.VMEM((2, 4, 8, nz), jnp.float32),
    ]
    result = jax.ShapeDtypeStruct((19, bx, by, nz), jnp.float32)
    slim = [(2, 5, by, nz), (2, 5, bx, nz), (4, 8, nz)]
    halos = [jax.ShapeDtypeStruct(shape, jnp.float32) for shape in slim]
    middle = pl.pallas_call(
        functools.partial(flow_kernel, nx, ny, capacity, parts),
        out_shape=[result] + halos,
        in_specs=[pl.BlockSpec(memory_space=pltpu.SMEM), pl.BlockSpec(memory_space=pltpu.VMEM)]
        + [pl.BlockSpec(memory_space=pl.ANY)] * 4,
        out_specs=[pl.BlockSpec(memory_space=pl.ANY)] * 4,
        scratch_shapes=[
            pltpu.VMEM((chunks, LANES), jnp.int32),
            pltpu.SMEM((chunks, LANES), jnp.int32),
            pltpu.VMEM((chunks, LANES), jnp.int32),
            pltpu.VMEM((n, LANES), jnp.int32),
            pltpu.VMEM((bx, by, nz), jnp.int32),
            pltpu.VMEM((parts, 19, held, nz), jnp.float32),
            tiles,
            tiles,
            pltpu.VMEM((n, chunks, LANES), jnp.int32),
            pltpu.VMEM((1, LANES), jnp.int32),
            pltpu.SMEM((1, LANES), jnp.int32),
            pltpu.SMEM((n, LANES), jnp.int32),
            pltpu.VMEM((capacity * parts, nz), jnp.float32),
            pltpu.VMEM((capacity * parts, nz), jnp.float32),
            pltpu.VMEM((capacity * parts, nz), jnp.int32),
            block,
            block,
            field,
            field,
        ]
        + faces
        + faces
        + [pltpu.SemaphoreType.DMA((n,))] * 4
        + [pltpu.SemaphoreType.DMA((2 * ny,))] * 2
        + [pltpu.SemaphoreType.DMA((parts + 6,))]
        + [pltpu.SemaphoreType.DMA((2, 8))] * 2,
        compiler_params=pltpu.CompilerParams(
            collective_id=0, has_side_effects=True, vmem_limit_bytes=62 * MIB
        ),
        name="exchange_and_flow",
    )(
        force,
        tile_target.reshape(1, held),
        jnp.transpose(pdf_old, (1, 0, 2)),
        porosity,
        relaxation,
        solid_mask,
    )
    pieces = 4
    return pl.pallas_call(
        functools.partial(finish_kernel, pieces),
        out_shape=result,
        in_specs=[pl.BlockSpec(memory_space=pl.ANY)] * 4,
        out_specs=pl.BlockSpec(memory_space=pl.ANY),
        scratch_shapes=[field, pltpu.VMEM((19, bx, by, nz), jnp.float32)]
        + [pltpu.VMEM(shape, jnp.float32) for shape in slim]
        + [pltpu.SemaphoreType.DMA((pieces,))] * 2
        + [pltpu.SemaphoreType.DMA((3,))],
        compiler_params=pltpu.CompilerParams(vmem_limit_bytes=62 * MIB),
        name="last_stream",
    )(*middle)


def solution(mesh):
    return jax.shard_map(
        local,
        mesh=mesh,
        in_specs=(
            P(("gx", "gy"), None, None),
            P(("gx", "gy")),
            P(("gx", "gy"), None, None),
            P(("gx", "gy"), None, None),
            P("gx", "gy", None),
            P(),
        ),
        out_specs=P(None, "gx", "gy", None),
        check_vma=False,
    )
```

```python
import functools

import jax
import jax.numpy as jnp
from jax import lax
from jax.experimental import pallas as pl
from jax.experimental.pallas import tpu as pltpu
from jax.sharding import PartitionSpec as P

STEPS = 2
VELOCITY = (
    (0, 0, 0),
    (1, 0, 0),
    (-1, 0, 0),
    (0, 1, 0),
    (0, -1, 0),
    (0, 0, 1),
    (0, 0, -1),
    (1, 1, 0),
    (-1, -1, 0),
    (1, -1, 0),
    (-1, 1, 0),
    (1, 0, 1),
    (-1, 0, -1),
    (1, 0, -1),
    (-1, 0, 1),
    (0, 1, 1),
    (0, -1, -1),
    (0, 1, -1),
    (0, -1, 1),
)
MAGIC = 0.1875
MESH = pl.DeviceIdType.MESH
LANES = 128
PAD = 8
MIB = 1 << 20


def moving(axis, sign):
    return [q for q in range(19) if VELOCITY[q][axis] == sign]


CORNERS = [(q, VELOCITY[q][0], VELOCITY[q][1]) for q in range(19) if VELOCITY[q][0] * VELOCITY[q][1] != 0]


def collide(dev, porosity, omega, mask, force):
    solid = porosity + mask.astype(jnp.float32) * (1.0 - porosity)
    fluid = 1.0 - solid
    omega_minus = (2.0 - omega) / (1.0 + (2.0 * MAGIC - 0.5) * omega)
    sums = {q: dev[q] + dev[q + 1] for q in range(1, 19, 2)}
    gaps = {q: dev[q] - dev[q + 1] for q in range(1, 19, 2)}
    axis_sum = sums[1] + sums[3] + sums[5]
    diagonal_sum = (sums[7] + sums[9]) + (sums[11] + sums[13]) + (sums[15] + sums[17])
    density = dev[0] * (1.0 / 3.0) + axis_sum * (1.0 / 18.0) + diagonal_sum * (1.0 / 36.0)
    flow = []
    for axis in range(3):
        straight = gaps[1 + 2 * axis]
        slanted = None
        for q in range(7, 19, 2):
            if VELOCITY[q][axis]:
                term = gaps[q] if VELOCITY[q][axis] > 0 else -gaps[q]
                slanted = term if slanted is None else slanted + term
        flow.append(straight * (1.0 / 18.0) + slanted * (1.0 / 36.0) + 0.5 * force[axis])
    base = density - 1.5 * (flow[0] * flow[0] + flow[1] * flow[1] + flow[2] * flow[2])
    pull = fluid * omega
    keep = 0.5 * (1.0 - pull)
    turn = 0.5 * (fluid * (1.0 - omega_minus) - solid)
    push = [3.0 * fluid * (omega_minus * flow[axis] + force[axis]) for axis in range(3)]

    def along(vector, velocity):
        total = None
        for axis in range(3):
            if velocity[axis]:
                term = vector[axis] if velocity[axis] > 0 else -vector[axis]
                total = term if total is None else total + term
        return total

    post = [None] * 19
    post[0] = dev[0] + pull * (base - dev[0])
    for q in range(1, 19, 2):
        speed = along(flow, VELOCITY[q])
        even = keep * sums[q] + pull * (base + 4.5 * (speed * speed))
        odd = turn * gaps[q] + along(push, VELOCITY[q])
        post[q] = even + odd
        post[q + 1] = even - odd
    return post


def column(rows, diagonal):
    return jnp.sum(jnp.where(diagonal, rows, 0), axis=1, keepdims=True)


def fill_tables(held, capacity, goal, table, labels):
    sub = lax.broadcasted_iota(jnp.int32, (held, LANES), 0)
    lane = lax.broadcasted_iota(jnp.int32, (held, LANES), 1)
    diagonal = sub == lane
    goals = jnp.broadcast_to(goal[...], (held, LANES))
    owners = lax.shift_right_logical(goals, held.bit_length() - 1)
    inner = goals - owners * held
    same = (column(owners, diagonal) == owners) & (sub < lane)
    rank = jnp.sum(jnp.where(same, 1, 0), axis=0, keepdims=True)
    slot = column(owners * capacity + rank, diagonal)
    place = column(inner, diagonal)
    for c in range(table.shape[0]):
        hit = slot == lane + c * LANES
        table[c : c + 1, :] = jnp.max(jnp.where(hit, sub, 0), axis=0, keepdims=True)
        labels[c : c + 1, :] = jnp.max(jnp.where(hit, place, -1), axis=0, keepdims=True)


def reach(bx, by):
    return {1: 0, -1: bx + 1}, {1: PAD - 1, -1: PAD + by}


def unpack_faces(field, x_face, y_face, c_face, bx, by):
    to_x, to_y = reach(bx, by)
    for i, sign in enumerate((1, -1)):
        for j, q in enumerate(moving(0, sign)):
            field[q, to_x[sign], PAD : PAD + by, :] = x_face[i, j]

    def spread(x, carry):
        for i, sign in enumerate((1, -1)):
            for j, q in enumerate(moving(1, sign)):
                field[q, x + 1, to_y[sign] : to_y[sign] + 1, :] = y_face[i, j, pl.ds(x, 1), :]
        return carry

    lax.fori_loop(0, bx, spread, 0)
    for i, (q, dx, dy) in enumerate(CORNERS):
        field[q, to_x[dx], to_y[dy] : to_y[dy] + 1, :] = c_face[i, 0:1, :]


def streamed(field, q, x, h):
    dx, dy, dz = VELOCITY[q]
    window = field[q, x + 1 - dx, PAD + h - dy : PAD + h - dy + 8, :]
    return pltpu.roll(window, dz % LANES, 1) if dz else window


def finish_kernel(pieces, middle, x_face, y_face, c_face, out, field, stage, x_in, y_in, c_in,
                  load_sem, store_sem, face_sem):
    bx, by = out.shape[1:3]
    size = bx // pieces
    loads = [
        pltpu.make_async_copy(
            middle.at[:, pl.ds(c * size, size)],
            field.at[:, pl.ds(1 + c * size, size), pl.ds(PAD, by), :],
            load_sem.at[c],
        )
        for c in range(pieces)
    ]
    stores = [
        pltpu.make_async_copy(
            stage.at[:, pl.ds(c * size, size)], out.at[:, pl.ds(c * size, size)], store_sem.at[c]
        )
        for c in range(pieces)
    ]
    faces = [
        pltpu.make_async_copy(face, ref, face_sem.at[i])
        for i, (face, ref) in enumerate(((x_face, x_in), (y_face, y_in), (c_face, c_in)))
    ]
    for copy in faces + loads:
        copy.start()
    for copy in faces:
        copy.wait()
    unpack_faces(field, x_in, y_in, c_in, bx, by)
    loads[0].wait()

    def plane(x, carry):
        for h in range(0, by, 8):
            for q in range(19):
                stage[q, x, h : h + 8, :] = streamed(field, q, x, h)
        return carry

    for c in range(pieces):
        if c + 1 < pieces:
            loads[c + 1].wait()
        lax.fori_loop(c * size, (c + 1) * size, plane, 0)
        stores[c].start()
    for store in stores:
        store.wait()


def flow_kernel(nx, ny, capacity, parts,
                force, goal, pdf, poro, relax, mask_hbm, middle, x_out, y_out, c_out,
                table_rows, table, labels, gathered, mask, halves, packed, arrived, places, slots,
                slot_of, label_of, plane, near_poro, near_relax, near_mask, poro_block, relax_block,
                first, second, x_send, y_send, c_send, x_recv, y_recv, c_recv,
                tile_send, tile_recv, label_send, label_recv, cell_send, cell_recv, own, send, recv):
    n = nx * ny
    held = pdf.shape[1]
    depth = capacity * parts
    a, b = lax.axis_index("gx"), lax.axis_index("gy")
    me = a * ny + b
    bx, by = mask.shape[:2]
    slab = poro.shape[0]
    half = nx // 2
    loads = [
        pltpu.make_async_copy(pdf.at[:, :, pl.ds(r * LANES, LANES)], halves.at[r], own.at[r])
        for r in range(parts)
    ]
    mine = [
        pltpu.make_async_copy(
            whole.at[:, pl.ds(b * by, by), :], block.at[pl.ds(b * slab, slab)], own.at[parts + i]
        )
        for i, (whole, block) in enumerate(((poro, poro_block), (relax, relax_block)))
    ]
    mine.append(pltpu.make_async_copy(mask_hbm, mask, own.at[parts + 2]))
    down = pltpu.make_async_copy(table_rows, table, own.at[parts + 3])
    for copy in loads + mine:
        copy.start()

    def partner(o, sign):
        side = 1 - lax.rem(o // (half * ny), 2)
        i = lax.rem(o // ny, half)
        j = lax.rem(o, ny)
        other = lax.rem(a // half + side, 2) * half + lax.rem(lax.rem(a, half) + half + sign * i, half)
        return other, lax.rem(b + ny + sign * j, ny)

    def order(step):
        pair = step // 2
        return pair + lax.rem(step, 2) * (n // 2 + 1)

    barrier = pltpu.get_barrier_semaphore()

    def greet(step, carry):
        pl.semaphore_signal(barrier, inc=1, device_id=partner(order(step), 1), device_id_type=MESH)
        return carry

    lax.fori_loop(0, n - 1, greet, 0)
    fill_tables(held, capacity, goal, table_rows, labels)
    down.start()
    down.wait()
    pl.semaphore_wait(barrier, n - 1)

    def label_copy(o, slot):
        return pltpu.make_async_remote_copy(
            src_ref=labels, dst_ref=places.at[slot],
            send_sem=label_send.at[o], recv_sem=label_recv.at[o],
            device_id=partner(o, 1), device_id_type=MESH,
        )

    def tile_copy(o, source, slot):
        return pltpu.make_async_remote_copy(
            src_ref=packed.at[source], dst_ref=arrived.at[slot],
            send_sem=tile_send.at[o], recv_sem=tile_recv.at[o],
            device_id=partner(o, 1), device_id_type=MESH,
        )

    def number(device):
        return device[0] * ny + device[1]

    def cell_copies(o, source, target):
        return [
            pltpu.make_async_remote_copy(
                src_ref=whole.at[:, pl.ds(target * by, by), :],
                dst_ref=block.at[pl.ds(source * slab, slab)],
                send_sem=cell_send.at[2 * o + i], recv_sem=cell_recv.at[2 * o + i],
                device_id=(a, target), device_id_type=MESH,
            )
            for i, (whole, block) in enumerate(((poro, poro_block), (relax, relax_block)))
        ]

    for copy in loads:
        copy.wait()
    flat = [halves.at[r].reshape(19 * held, LANES) for r in range(parts)]

    def fill(block, goal):
        for k in range(capacity):
            spot = goal * capacity + k
            tile = table[spot // LANES, lax.rem(spot, LANES)]
            for r in range(parts):
                block[goal if block is packed else me, pl.ds(k * parts + r, 19, stride=depth), :] = (
                    flat[r][pl.ds(tile, 19, stride=held), :]
                )

    def send_tiles(step, carry):
        o = order(step)
        goal_device = number(partner(o, 1))
        fill(packed, goal_device)
        tile_copy(o, goal_device, me).start()
        return carry

    def send_labels(step, carry):
        label_copy(order(step), me).start()
        return carry

    lax.fori_loop(0, n - 1, send_labels, 0)
    lax.fori_loop(0, n - 1, send_tiles, 0)
    for o in range(1, ny):
        for copy in cell_copies(o, b, lax.rem(b + o, ny)):
            copy.start()
    fill(arrived, me)
    places[me] = labels[...]
    for copy in mine:
        copy.wait()
    for o in range(1, ny):
        for copy in cell_copies(o, lax.rem(b + ny - o, ny), lax.rem(b + o, ny)):
            copy.wait_send()
            copy.wait_recv()

    def take_labels(step, carry):
        o = order(step)
        label_copy(o, number(partner(o, -1))).wait_recv()
        return carry

    lax.fori_loop(0, n - 1, take_labels, 0)
    chunk, offset = (me * capacity) // LANES, lax.rem(me * capacity, LANES)

    def collect(d, carry):
        gathered[pl.ds(d, 1), :] = places[d, pl.ds(chunk, 1), :]
        return carry

    lax.fori_loop(0, n, collect, 0)
    rows = gathered[...]
    sender = lax.broadcasted_iota(jnp.int32, (n, LANES), 0)
    lane = lax.broadcasted_iota(jnp.int32, (n, LANES), 1)
    found = jnp.zeros((n, LANES), jnp.int32)
    for k in range(capacity):
        label = jnp.sum(jnp.where(lane == offset + k, rows, 0), axis=1, keepdims=True)
        found = jnp.maximum(found, jnp.where(label == lane, sender * capacity + k, 0))
    slots[...] = jnp.max(found, axis=0, keepdims=True)
    lift = pltpu.make_async_copy(slots, slot_of, own.at[parts + 4])
    spread_out = pltpu.make_async_copy(gathered, label_of, own.at[parts + 5])
    lift.start()
    spread_out.start()
    lift.wait()
    spread_out.wait()
    forces = [force[axis] for axis in range(3)]
    strips = by // parts
    cell_rows = [ref.reshape(bx * by, LANES) for ref in (poro_block, relax_block, mask)]
    size = min(8, depth)

    def collide_block(source):
        for k in range(capacity):
            begin = jnp.maximum(label_of[source, offset + k], 0) * parts
            for rows_of, near in zip(cell_rows, (near_poro, near_relax, near_mask)):
                near[k * parts : (k + 1) * parts, :] = rows_of[pl.ds(begin, parts), :]
        for h in range(0, depth, size):
            dev = [arrived[source, q * depth + h : q * depth + h + size, :] for q in range(19)]
            near = [ref[h : h + size, :] for ref in (near_poro, near_relax, near_mask)]
            done = collide(dev, *near, forces)
            for q in range(19):
                arrived[source, q * depth + h : q * depth + h + size, :] = done[q]

    collide_block(me)

    def take_tiles(step, carry):
        o = order(step)
        source = number(partner(o, -1))
        tile_copy(o, source, source).wait_recv()
        collide_block(source)
        return carry

    lax.fori_loop(0, n - 1, take_tiles, 0)
    tall = by + 2 * PAD
    first_rows = first.reshape(19 * (bx + 2) * tall, LANES)

    def start(x, carry):
        for j in range(strips):
            slot = slot_of[0, x * strips + j]
            source = lax.div(slot, capacity)
            row = (slot - source * capacity) * parts
            for r in range(parts):
                plane[pl.ds(j * parts + r, 19, stride=by), :] = arrived[
                    source, pl.ds(row + r, 19, stride=depth), :
                ]
        for q in range(19):
            first[q, x + 1, PAD : PAD + by, :] = plane[q * by : (q + 1) * by, :]
        return carry

    lax.fori_loop(0, bx, start, 0)

    ring_x = {1: lax.rem(a + 1, nx), -1: lax.rem(a + nx - 1, nx), 0: a}
    ring_y = {1: lax.rem(b + 1, ny), -1: lax.rem(b + ny - 1, ny), 0: b}
    from_x, from_y = {1: bx, -1: 1}, {1: PAD + by - 1, -1: PAD}

    def copies(turn):
        plan = [(x_send, x_recv, i, (sign, 0)) for i, sign in enumerate((1, -1))]
        plan += [(y_send, y_recv, i, (0, sign)) for i, sign in enumerate((1, -1))]
        plan += [(c_send, c_recv, i, (dx, dy)) for i, (q, dx, dy) in enumerate(CORNERS)]
        return [
            pltpu.make_async_remote_copy(
                src_ref=source.at[turn, i], dst_ref=goal.at[turn, i],
                send_sem=send.at[turn, k], recv_sem=recv.at[turn, k],
                device_id=(ring_x[dx], ring_y[dy]), device_id_type=MESH,
            )
            for k, (source, goal, i, (dx, dy)) in enumerate(plan)
        ]

    def send_faces(turn, field):
        for i, sign in enumerate((1, -1)):
            for j, q in enumerate(moving(0, sign)):
                x_send[turn, i, j] = field[q, from_x[sign], PAD : PAD + by, :]

        def gather(x, carry):
            for i, sign in enumerate((1, -1)):
                for j, q in enumerate(moving(1, sign)):
                    y_send[turn, i, j, pl.ds(x, 1), :] = field[
                        q, x + 1, from_y[sign] : from_y[sign] + 1, :
                    ]
            return carry

        lax.fori_loop(0, bx, gather, 0)
        for i, (q, dx, dy) in enumerate(CORNERS):
            c_send[turn, i, 0:1, :] = field[q, from_x[dx], from_y[dy] : from_y[dy] + 1, :]
        for move in copies(turn):
            move.start()

    def take_faces(turn, field):
        for move in copies(turn):
            move.wait()
        unpack_faces(field, x_recv.at[turn], y_recv.at[turn], c_recv.at[turn], bx, by)

    def block(x, h):
        dev = [streamed(first, q, x, h) for q in range(19)]
        done = collide(
            dev, poro_block[x, h : h + 8], relax_block[x, h : h + 8], mask[x, h : h + 8], forces
        )
        for q in range(19):
            second[q, x + 1, PAD + h : PAD + h + 8, :] = done[q]

    def second_step(x, carry):
        for h in range(0, by, 8):
            block(x, h)
        return carry

    second_rows = second.reshape(19 * (bx + 2) * tall, LANES)

    def edge(row, x):
        dev = []
        for q in range(19):
            dx, dy, dz = VELOCITY[q]
            begin = (q * (bx + 2) + x + 1 - dx) * tall + PAD + row - dy
            window = first_rows[pl.ds(begin, 8, stride=tall), :]
            dev.append(pltpu.roll(window, dz % LANES, 1) if dz else window)
        cells = [ref[pl.ds(x * by + row, 8, stride=by), :] for ref in cell_rows]
        done = collide(dev, *cells, forces)
        for q in range(19):
            begin = (q * (bx + 2) + x + 1) * tall + PAD + row
            second_rows[pl.ds(begin, 8, stride=tall), :] = done[q]

    send_faces(0, first)
    lax.fori_loop(1, bx - 1, second_step, 0)
    take_faces(0, first)
    for x in (0, bx - 1):
        second_step(x, 0)
    for x in range(0, bx, 8):
        for row in (0, by - 1):
            edge(row, x)
    keep = pltpu.make_async_copy(
        second.at[:, pl.ds(1, bx), pl.ds(PAD, by), :], middle, own.at[0]
    )
    keep.start()
    send_faces(1, second)
    for move in copies(1):
        move.wait()
    faces = [
        pltpu.make_async_copy(ref.at[1], face, own.at[1 + i])
        for i, (ref, face) in enumerate(((x_recv, x_out), (y_recv, y_out), (c_recv, c_out)))
    ]
    for copy in faces:
        copy.start()
    for copy in faces:
        copy.wait()
    keep.wait()

    def sent(step, carry):
        o = order(step)
        label_copy(o, me).wait_send()
        tile_copy(o, number(partner(o, 1)), me).wait_send()
        return carry

    lax.fori_loop(0, n - 1, sent, 0)


def local(pdf_old, tile_target, porosity, relaxation, solid_mask, force):
    nx, ny = lax.axis_size("gx"), lax.axis_size("gy")
    n = nx * ny
    held, _, tile_cells = pdf_old.shape
    capacity = 2 * held // n
    bx, by, nz = solid_mask.shape
    parts = tile_cells // nz
    chunks = n * capacity // LANES
    tiles = pltpu.VMEM((n, 19 * capacity * parts, nz), jnp.float32)
    block = pltpu.VMEM((bx, by, nz), jnp.float32)
    field = pltpu.VMEM((19, bx + 2, by + 2 * PAD, nz), jnp.float32)
    faces = [
        pltpu.VMEM((2, 2, 5, by, nz), jnp.float32),
        pltpu.VMEM((2, 2, 5, bx, nz), jnp.float32),
        pltpu.VMEM((2, 4, 8, nz), jnp.float32),
    ]
    result = jax.ShapeDtypeStruct((19, bx, by, nz), jnp.float32)
    slim = [(2, 5, by, nz), (2, 5, bx, nz), (4, 8, nz)]
    halos = [jax.ShapeDtypeStruct(shape, jnp.float32) for shape in slim]
    middle = pl.pallas_call(
        functools.partial(flow_kernel, nx, ny, capacity, parts),
        out_shape=[result] + halos,
        in_specs=[pl.BlockSpec(memory_space=pltpu.SMEM), pl.BlockSpec(memory_space=pltpu.VMEM)]
        + [pl.BlockSpec(memory_space=pl.ANY)] * 4,
        out_specs=[pl.BlockSpec(memory_space=pl.ANY)] * 4,
        scratch_shapes=[
            pltpu.VMEM((chunks, LANES), jnp.int32),
            pltpu.SMEM((chunks, LANES), jnp.int32),
            pltpu.VMEM((chunks, LANES), jnp.int32),
            pltpu.VMEM((n, LANES), jnp.int32),
            pltpu.VMEM((bx, by, nz), jnp.int32),
            pltpu.VMEM((parts, 19, held, nz), jnp.float32),
            tiles,
            tiles,
            pltpu.VMEM((n, chunks, LANES), jnp.int32),
            pltpu.VMEM((1, LANES), jnp.int32),
            pltpu.SMEM((1, LANES), jnp.int32),
            pltpu.SMEM((n, LANES), jnp.int32),
            pltpu.VMEM((19 * by, nz), jnp.float32),
            pltpu.VMEM((capacity * parts, nz), jnp.float32),
            pltpu.VMEM((capacity * parts, nz), jnp.float32),
            pltpu.VMEM((capacity * parts, nz), jnp.int32),
            block,
            block,
            field,
            field,
        ]
        + faces
        + faces
        + [pltpu.SemaphoreType.DMA((n,))] * 4
        + [pltpu.SemaphoreType.DMA((2 * ny,))] * 2
        + [pltpu.SemaphoreType.DMA((parts + 6,))]
        + [pltpu.SemaphoreType.DMA((2, 8))] * 2,
        compiler_params=pltpu.CompilerParams(
            collective_id=0, has_side_effects=True, vmem_limit_bytes=62 * MIB
        ),
        name="exchange_and_flow",
    )(
        force,
        tile_target.reshape(1, held),
        jnp.transpose(pdf_old, (1, 0, 2)),
        porosity,
        relaxation,
        solid_mask,
    )
    pieces = 4
    return pl.pallas_call(
        functools.partial(finish_kernel, pieces),
        out_shape=result,
        in_specs=[pl.BlockSpec(memory_space=pl.ANY)] * 4,
        out_specs=pl.BlockSpec(memory_space=pl.ANY),
        scratch_shapes=[field, pltpu.VMEM((19, bx, by, nz), jnp.float32)]
        + [pltpu.VMEM(shape, jnp.float32) for shape in slim]
        + [pltpu.SemaphoreType.DMA((pieces,))] * 2
        + [pltpu.SemaphoreType.DMA((3,))],
        compiler_params=pltpu.CompilerParams(vmem_limit_bytes=62 * MIB),
        name="last_stream",
    )(*middle)


def solution(mesh):
    return jax.shard_map(
        local,
        mesh=mesh,
        in_specs=(
            P(("gx", "gy"), None, None),
            P(("gx", "gy")),
            P(("gx", "gy"), None, None),
            P(("gx", "gy"), None, None),
            P("gx", "gy", None),
            P(),
        ),
        out_specs=P(None, "gx", "gy", None),
        check_vma=False,
    )
```
